256 devices in a mesh: row: 32 (over z, x), col: 8 (over y, core).
Axes of the slice: x: 4, y: 4, z: 8, core: 2. Of those that a mesh axis runs over, the one named last changes fastest.
Arguments:
- head_start: bfloat16 [512, 1024, 128], P('row', 'col'), may hold values from -6 to 6
- cotangent: bfloat16 [512, 1024, 128], P('row', 'col'), may hold values from -6 to 6
- conductivity: bfloat16 [512, 1024, 128], P('row', 'col'), may hold values from 0.19921875 to 2
- line_x: bfloat16 [512, 512], replicated, may hold values from -1 to 1.5
- line_y: bfloat16 [1024, 1024], replicated, may hold values from -1 to 1.5
- line_z: bfloat16 [128, 128], replicated, may hold values from -1 to 1.5
- zone_map: int32 [512, 1024], replicated, may hold values from 0 to 2047
- owner_order: int32 [2048], replicated, may hold values from 0 to 2047, each once
Outputs:
- head_adjoint: bfloat16 [512, 1024, 128], P('row', 'col')
- zone_grad: float32 [2048], P(('row', 'col'))
The draws below stay inside these ranges and needn't reach their ends.
All inputs are finite; a program needn't handle non-finite values.
Results may differ from the reference program's by a relative error of at most 0.007.
Values may be sent and summed in bfloat16 or wider, within the bound.
A program may use at most 64 MiB of HBM per device.

```python
import math
import jax
import jax.numpy as jnp
from jax import lax

NZ = 128
STEPS = 2
NX = 512
NY = 1024
ZONES = 2048


def assemble_line(noise, length):
    return (0.8 * jnp.eye(length, dtype=jnp.float32) + 0.5 * noise / math.sqrt(length)).astype(jnp.bfloat16)


def draw_line_x(key, part):
    key = jax.random.fold_in(key, 11)
    noise = jnp.clip(jax.random.normal(key, (NX, NX), jnp.float32), -4.0, 4.0)
    return assemble_line(noise, NX)


def draw_line_y(key, part):
    key = jax.random.fold_in(key, 12)
    noise = jnp.clip(jax.random.normal(key, (NY, NY), jnp.float32), -4.0, 4.0)
    return assemble_line(noise, NY)


def draw_line_z(key, part):
    key = jax.random.fold_in(key, 13)
    noise = jnp.clip(jax.random.normal(key, (NZ, NZ), jnp.float32), -4.0, 4.0)
    return assemble_line(noise, NZ)


def set_ends(entries, rng, least, top_value):
    dims = entries.shape
    spot = [jax.random.randint(jax.random.fold_in(rng, axis), (), 0, dims[axis]) for axis in range(len(dims))]
    entries = entries.at[tuple(spot)].set(least)
    longest = dims.index(max(dims))
    spot[longest] = (spot[longest] + 1) % dims[longest]
    return entries.at[tuple(spot)].set(top_value)


def shard_levels(stream_key, dims, shards, low, top_value):
    level = 1.0
    for axis_at, blocks in shards:
        steps = jax.random.uniform(jax.random.fold_in(jax.random.fold_in(stream_key, 6), axis_at), (blocks,), jnp.float32, low / len(shards), top_value / len(shards))
        level = level * jnp.repeat(jnp.exp(steps), dims[axis_at] // blocks).reshape((-1,) + (1,) * (len(dims) - 1 - axis_at))
    return level


def scatter_about(stream_key, shape, spread, most, cuts=(), kind=jnp.bfloat16):
    entries = spread * jax.random.normal(stream_key, shape, jnp.float32)
    if cuts:
        entries = entries * shard_levels(stream_key, shape, cuts, -0.22, 0.18)
    return jnp.clip(entries, -most, most).astype(kind)


def setup_inputs(seed: int = 0) -> dict:
    splits = jax.random.split(jax.random.key(seed), 9)
    head_start = scatter_about(splits[0], (NX, NY, NZ), 1.0, 6.0, ((0, 32), (1, 8)))
    cotangent = scatter_about(splits[1], (NX, NY, NZ), 1.0, 6.0, ((0, 32), (1, 8)))
    conductivity = jnp.clip(jnp.exp(math.log(2.0) - 2.306499 * jax.random.uniform(splits[2], (NX, NY, NZ), jnp.float32) ** shard_levels(splits[2], (NX, NY, NZ), ((0, 32), (1, 8)), -0.2, 0.2)), 0.19921875, 2.0).astype(jnp.bfloat16)
    line_x = draw_line_x(jax.random.fold_in(splits[8], 71), 0)
    line_y = draw_line_y(jax.random.fold_in(splits[8], 71), 0)
    line_z = draw_line_z(jax.random.fold_in(splits[8], 71), 0)
    zone_map = set_ends(jax.random.randint(splits[6], (NX, NY), 0, ZONES), jax.random.fold_in(splits[6], 1), 0, ZONES - 1).astype(jnp.int32)
    owner_order = jax.random.permutation(splits[7], ZONES).astype(jnp.int32)
    return {"head_start": head_start, "cotangent": cotangent, "conductivity": conductivity, "line_x": line_x, "line_y": line_y, "line_z": line_z, "zone_map": zone_map, "owner_order": owner_order}


time_step = 0.15

def pad_side(values, direction, before):
    widths = [(0, 0)] * values.ndim
    widths[direction] = (before, 1 - before)
    return jnp.pad(values, widths)

def flux_divergence(heads, conduct, direction):
    length = heads.shape[direction]
    deltas = jnp.diff(heads, axis=direction)
    face_cond = 0.5 * (lax.slice_in_dim(conduct, 0, length - 1, axis=direction) + lax.slice_in_dim(conduct, 1, length, axis=direction))
    fluxes = face_cond * deltas
    return pad_side(fluxes, direction, 0) - pad_side(fluxes, direction, 1)

def flux_product(states, backed, direction):
    products = jnp.diff(states, axis=direction) * jnp.diff(backed, axis=direction)
    return -0.5 * time_step * (pad_side(products, direction, 0) + pad_side(products, direction, 1))

def line_apply(matrix, source, direction, transpose):
    length = matrix.shape[0]
    if direction == 0:
        operator = matrix.T if transpose else matrix
        return jnp.dot(operator, source.reshape(length, -1), preferred_element_type=jnp.float32).reshape(source.shape)
    if direction == 1:
        pattern = 'ji,ajb->aib' if transpose else 'ij,ajb->aib'
        return jnp.einsum(pattern, matrix.astype(jnp.float32), source.astype(jnp.float32), precision=lax.Precision.HIGHEST)
    operator = matrix if transpose else matrix.T
    return jnp.dot(source.reshape(-1, length), operator, preferred_element_type=jnp.float32).reshape(source.shape)

def reference(head_start, cotangent, conductivity, line_x, line_y, line_z, zone_map, owner_order):
    conduct = conductivity.astype(jnp.float32)
    matrices = (line_x, line_y, line_z)
    section_total = 3 * STEPS
    stored = []
    heads = head_start
    for section_index in range(section_total):
        direction = section_index % 3
        stored.append(heads)
        if section_index + 1 < section_total:
            widened = heads.astype(jnp.float32)
            source = (widened + time_step * flux_divergence(widened, conduct, direction)).astype(jnp.bfloat16)
            heads = line_apply(matrices[direction], source, direction, False).astype(jnp.bfloat16)
    adjoint = cotangent
    column_grad = jnp.zeros((NX, NY), jnp.float32)
    for section_index in reversed(range(section_total)):
        direction = section_index % 3
        backed = line_apply(matrices[direction], adjoint, direction, True)
        column_grad = column_grad + lax.optimization_barrier(jnp.sum(flux_product(stored[section_index].astype(jnp.float32), backed, direction), axis=2))
        adjoint = (backed + time_step * flux_divergence(backed, conduct, direction)).astype(jnp.bfloat16)
    zone_sums = jax.ops.segment_sum(column_grad.reshape(-1), zone_map.reshape(-1), num_segments=ZONES)
    return (adjoint, zone_sums[owner_order] / math.sqrt(NX * NY * NZ / ZONES))
```

```python
import functools
import math

import jax
import jax.numpy as jnp
from jax import lax
from jax.experimental import pallas as pl
from jax.experimental.pallas import tpu as pltpu
from jax.sharding import PartitionSpec as P

MESH = pl.DeviceIdType.MESH
BF = jnp.bfloat16
F32 = jnp.float32
HALF_STEP = 0.075
PAD = 8


def dot_nn(a, b):
    return lax.dot_general(a, b, (((1,), (0,)), ((), ())), preferred_element_type=F32)


def dot_nt(a, b):
    return lax.dot_general(a, b, (((1,), (1,)), ((), ())), preferred_element_type=F32)


def dot_tn(a, b):
    return lax.dot_general(a, b, (((0,), (0,)), ((), ())), preferred_element_type=F32)


def loop(count, body, unroll=1):
    def step(i, carry):
        body(i)
        return carry

    lax.fori_loop(0, count, step, 0, unroll=unroll)


def split_two(values):
    high = values.astype(BF)
    low = (values - high.astype(F32)).astype(BF)
    return high, low


def kernel(
    rows, cols, scale,
    head_hbm, cot_hbm, cond_hbm, lx_hbm, ly_hbm, lz_hbm, zmap_hbm, owner_hbm,
    out_ref, zout_ref,
    head, cond, state3, back3, back0, cot, lx, ly, lz, zone_s, zone_y, zone_lines, owner,
    rs, rr, cs, cr, turn, cfx, cfz_s, cfy, cfz_y,
    field1, field4, grad4, grad1, back5, src_y,
    q_y, v_s, v_y, lo_s, lo_y, lo_own, zacc, z_send, z_mid, z_row, z_col,
    local_sem, rs_sem, rr_sem, cs_sem, cr_sem, hs_sem, hr_sem, zs_sem, zr_sem,
):
    row = lax.axis_index("row")
    col = lax.axis_index("col")
    slab_x, slab_y, depth = head_hbm.shape
    part_y = slab_y // rows
    part_x = slab_x // cols
    total_x = lx.shape[0]
    total_y = ly.shape[0]

    def row_peer(i):
        return lax.rem(row + i, rows)

    def col_peer(i):
        return lax.rem(col + i, cols)

    loads = {}

    def load(slot, src, dst):
        copy = pltpu.make_async_copy(src, dst, local_sem.at[slot])
        copy.start()
        loads[slot] = copy

    inner = pl.ds(1, slab_x)
    load(0, head_hbm, head.at[inner])
    load(1, cond_hbm, cond.at[inner])
    load(2, cot_hbm, cot)
    load(3, lz_hbm, lz)
    load(4, lx_hbm, lx)
    load(5, ly_hbm, ly)
    load(6, zmap_hbm.at[pl.ds(row * slab_x, slab_x), pl.ds(col * slab_y, slab_y)], zone_s)
    load(7, zmap_hbm.at[pl.ds(row * slab_x + (col * part_x // 8) * 8, 8)], zone_y)
    load(8, owner_hbm, owner)

    barrier = pltpu.get_barrier_semaphore()

    def greet_row(i):
        pl.semaphore_signal(barrier, inc=1, device_id=(row_peer(i + 1), col), device_id_type=MESH)

    def greet_col(i):
        pl.semaphore_signal(barrier, inc=1, device_id=(row, col_peer(i + 1)), device_id_type=MESH)

    loop(rows - 1, greet_row)
    loop(cols - 1, greet_col)
    pl.semaphore_wait(barrier, rows + cols - 2)

    def send_row(k):
        def one(i):
            r = row_peer(i + 1)
            pltpu.make_async_remote_copy(
                src_ref=rs.at[k, r], dst_ref=rr.at[k, row],
                send_sem=rs_sem.at[k], recv_sem=rr_sem.at[k],
                device_id=(r, col), device_id_type=MESH,
            ).start()

        loop(rows - 1, one)
        rr[k, row] = rs[k, row]

    def row_wait(k):
        part = pl.ds(0, rows - 1)
        return pltpu.make_async_remote_copy(
            src_ref=rs.at[k, part], dst_ref=rr.at[k, part],
            send_sem=rs_sem.at[k], recv_sem=rr_sem.at[k],
            device_id=(row, col), device_id_type=MESH,
        )

    def send_col(j, src, offset):
        def one(i):
            c = col_peer(i + 1)
            pltpu.make_async_remote_copy(
                src_ref=src.at[pl.ds(offset + c * part_x, part_x)],
                dst_ref=cr.at[j, pl.ds(col * part_x, part_x)],
                send_sem=cs_sem.at[j], recv_sem=cr_sem.at[j],
                device_id=(row, c), device_id_type=MESH,
            ).start()

        loop(cols - 1, one)
        cr[j, pl.ds(col * part_x, part_x)] = src[pl.ds(offset + col * part_x, part_x)]

    def col_wait(j):
        part = pl.ds(0, (cols - 1) * part_x)
        return pltpu.make_async_remote_copy(
            src_ref=cr.at[j, part], dst_ref=cr.at[j, part],
            send_sem=cs_sem.at[j], recv_sem=cr_sem.at[j],
            device_id=(row, col), device_id_type=MESH,
        )

    def halo_copies(h, buf):
        up = lax.rem(row + 1, rows)
        down = lax.rem(row + rows - 1, rows)
        return (
            pltpu.make_async_remote_copy(
                src_ref=buf.at[slab_x], dst_ref=buf.at[0],
                send_sem=hs_sem.at[h, 0], recv_sem=hr_sem.at[h, 0],
                device_id=(up, col), device_id_type=MESH,
            ),
            pltpu.make_async_remote_copy(
                src_ref=buf.at[1], dst_ref=buf.at[slab_x + 1],
                send_sem=hs_sem.at[h, 1], recv_sem=hr_sem.at[h, 1],
                device_id=(down, col), device_id_type=MESH,
            ),
        )

    def send_halo(h, buf):
        for copy in halo_copies(h, buf):
            copy.start()

    def wait_halo(h, buf):
        for copy in halo_copies(h, buf):
            copy.wait_recv()

    def next_lane(f):
        return pltpu.roll(f, f.shape[1] - 1, axis=1)

    def prev_lane(f):
        return pltpu.roll(f, 1, axis=1)

    def apply_z(f, faces):
        flux = faces * (next_lane(f) - f)
        return f + flux - prev_lane(flux)

    def lane_mask(shape):
        lane = lax.broadcasted_iota(jnp.int32, shape, 1)
        return jnp.where(lane < depth - 1, 1.0, 0.0).astype(F32)

    def plane_x(buf, x):
        below = buf[x].astype(F32)
        mid = buf[x + 1].astype(F32)
        above = buf[x + 2].astype(F32)
        return mid + cfx[x + 1] * (above - mid) - cfx[x] * (mid - below)

    ones8 = jnp.ones((8, depth), BF)

    def depth_sum(products):
        high, low = split_two(products)
        return dot_nt(ones8, high) + dot_nt(ones8, low)

    def turn_in(x, plane):
        turn[pl.ds(x, slab_y, stride=slab_x), :] = plane

    def turn_out(x):
        return turn[pl.ds(x, slab_y, stride=slab_x), :]

    block = part_y * slab_x

    def turned_to_send(k):
        def one(r):
            piece = turn[pl.ds(pl.multiple_of(r * block, block), block), :]
            rs[k, r] = piece.astype(BF).reshape(part_y, slab_x, depth)

        loop(rows, one, 4)

    def received_to_turn(k):
        def one(r):
            piece = rr[k, r].reshape(block, depth).astype(F32)
            turn[pl.ds(pl.multiple_of(r * block, block), block), :] = piece

        loop(rows, one, 4)

    x_chunk = 128
    peers_chunk = x_chunk // slab_x

    def line_x_step(k_in, k_out, transpose):
        rhs = jnp.concatenate(
            [rr[k_in, :, y].reshape(total_x, depth) for y in range(part_y)], axis=1
        )

        def one(m):
            part = pl.ds(pl.multiple_of(m * x_chunk, x_chunk), x_chunk)
            if transpose:
                res = dot_tn(lx[:, part], rhs)
            else:
                res = dot_nn(lx[part, :], rhs)
            res = res.astype(BF)
            for y in range(part_y):
                piece = res[:, y * depth:(y + 1) * depth].reshape(peers_chunk, slab_x, depth)
                rs[k_out, pl.ds(m * peers_chunk, peers_chunk), y] = piece

        loop(total_x // x_chunk, one)

    y_chunk = 256

    def line_y_chunk(m, transpose):
        part = pl.ds(pl.multiple_of(m * y_chunk, y_chunk), y_chunk)
        if transpose:
            return dot_tn(ly[:, part], src_y[...])
        return dot_nn(ly[part, :], src_y[...])

    def line_y_to_field(field, transpose):
        def one(m):
            res = line_y_chunk(m, transpose)
            for x in range(part_x):
                field[x, pl.ds(pl.multiple_of(PAD + m * y_chunk, 8), y_chunk), :] = res[
                    :, x * depth:(x + 1) * depth
                ]

        loop(total_y // y_chunk, one)
        pad_field(field)

    def pad_field(field):
        for x in range(part_x):
            field[x, 0:PAD, :] = jnp.zeros((PAD, depth), F32)
            field[x, PAD + total_y:, :] = jnp.broadcast_to(
                field[x, PAD + total_y - 1:PAD + total_y, :], (PAD, depth)
            )

    def received_to_field(j, field):
        def one(c):
            for x in range(part_x):
                field[x, pl.ds(pl.multiple_of(PAD + c * slab_y, 8), slab_y), :] = cr[
                    j, c * part_x + x
                ].astype(F32)

        loop(cols, one, 2)
        pad_field(field)

    def apply_y(field, x, c):
        base = pl.multiple_of(PAD + c * slab_y, 8)
        mid = field[x, pl.ds(base, slab_y), :]
        above = field[x, pl.ds(base + 1, slab_y), :]
        below = field[x, pl.ds(base - 1, slab_y), :]
        face = cfy[x, pl.ds(base, slab_y), :]
        face_below = cfy[x, pl.ds(base - 1, slab_y), :]
        return mid + face * (above - mid) - face_below * (mid - below)

    def grad_y(field, grad, x, c):
        base = pl.multiple_of(PAD + c * slab_y, 8)
        first = field[x, pl.ds(base + 1, slab_y), :] - field[x, pl.ds(base, slab_y), :]
        second = grad[x, pl.ds(base + 1, slab_y), :] - grad[x, pl.ds(base, slab_y), :]
        return depth_sum(first * second)

    def set_src_y(x, c, values):
        src_y[pl.ds(pl.multiple_of(c * slab_y, slab_y), slab_y), x * depth:(x + 1) * depth] = (
            values.astype(BF)
        )

    def low_codes(zones):
        code = jnp.broadcast_to(zones & (depth - 1), (depth, depth))
        return jnp.where(
            code == lax.broadcasted_iota(jnp.int32, (depth, depth), 0), 1.0, 0.0
        ).astype(BF)

    def high_codes(zones):
        code = jnp.broadcast_to(zones // depth, (16, depth))
        return jnp.where(code == lax.broadcasted_iota(jnp.int32, (16, depth), 0), 1.0, 0.0)

    def zone_add(values, zones, codes):
        spread = jnp.concatenate([values, values], axis=0) * high_codes(zones)
        high, low = split_two(spread)
        zacc[...] += dot_nt(jnp.concatenate([high, low], axis=0), codes)

    def zone_s_row(x):
        return zone_s[pl.ds(x, 1), :]

    def zone_y_row(x, c):
        return zone_lines[pl.ds(c * part_x + x, 1), :]

    def pick_zone_lines():
        groups = 8 // part_x
        for x in range(part_x):
            line = jnp.zeros((1, total_y), jnp.int32)
            for g in range(groups):
                mine = jnp.where(lax.rem(col, groups) == g, 1, 0)
                line = line + mine * zone_y[g * part_x + x:g * part_x + x + 1, :]
            for c in range(cols):
                zone_lines[c * part_x + x:c * part_x + x + 1, :] = line[
                    :, c * slab_y:(c + 1) * slab_y
                ]

    loads[0].wait()
    loads[1].wait()
    send_halo(0, head)
    send_halo(1, cond)
    loads[2].wait()
    send_col(1, cot, 0)
    send_col(0, cond, 1)
    loads[3].wait()

    def faces_z_slab(x):
        c = cond[1 + x].astype(F32)
        cfz_s[x] = HALF_STEP * (c + next_lane(c)) * lane_mask(c.shape)

    loop(slab_x, faces_z_slab, 2)

    wait_halo(1, cond)

    def faces_x_slab(j):
        at_end = ((j == 0) & (row == 0)) | ((j == slab_x) & (row == rows - 1))
        keep = jnp.where(at_end, 0.0, HALF_STEP).astype(F32)
        cfx[j] = keep * (cond[j].astype(F32) + cond[j + 1].astype(F32))

    loop(slab_x + 1, faces_x_slab)
    wait_halo(0, head)

    def first_source(x):
        turn_in(x, plane_x(head, x))

    loop(slab_x, first_source, 2)
    turned_to_send(0)
    send_row(0)

    zacc[...] = jnp.zeros(zacc.shape, F32)
    col_wait(0).wait_recv()

    def cond_lines(c):
        for x in range(part_x):
            own = cr[0, c * part_x + x].astype(F32)
            cfz_y[c * part_x + x] = HALF_STEP * (own + next_lane(own)) * lane_mask(own.shape)

    loop(cols, cond_lines)
    received_to_field(0, field1)

    def faces_y(c):
        for x in range(part_x):
            base = pl.multiple_of(PAD + c * slab_y, 8)
            cfy[x, pl.ds(base, slab_y), :] = HALF_STEP * (
                field1[x, pl.ds(base, slab_y), :] + field1[x, pl.ds(base + 1, slab_y), :]
            )

    loop(cols, faces_y)
    for x in range(part_x):
        cfy[x, 0:PAD, :] = jnp.zeros((PAD, depth), F32)
        cfy[x, PAD + total_y - 1:PAD + total_y, :] = jnp.zeros((1, depth), F32)
        cfy[x, PAD + total_y:, :] = jnp.zeros((PAD, depth), F32)

    col_wait(1).wait_recv()

    def adjoint5(c):
        for x in range(part_x):
            backed = dot_nn(cr[1, c * part_x + x], lz[...])
            back5[c * part_x + x] = backed
            set_src_y(x, c, apply_z(backed, cfz_y[c * part_x + x]))

    loop(cols, adjoint5)
    loads[5].wait()
    line_y_to_field(grad4, True)

    def adjoint4(c):
        for x in range(part_x):
            cs[0, c * part_x + x] = apply_y(grad4, x, c).astype(BF)

    loop(cols, adjoint4)
    send_col(2, cs.at[0], 0)

    loads[4].wait()
    row_wait(0).wait_recv()
    line_x_step(0, 1, False)
    send_row(1)

    col_wait(2).wait_recv()

    def adjoint4_turn(x):
        turn_in(x, cr[2, x].astype(F32))

    loop(slab_x, adjoint4_turn, 2)
    turned_to_send(2)
    send_row(2)

    loads[6].wait()
    loads[7].wait()
    loads[8].wait()

    def codes_s(x):
        lo_s[x] = low_codes(zone_s_row(x))

    def codes_y(c):
        for x in range(part_x):
            lo_y[c * part_x + x] = low_codes(zone_y_row(x, c))

    def codes_own(g):
        lo_own[g] = low_codes(owner[pl.ds(g, 1), :])

    pick_zone_lines()
    loop(slab_x, codes_s)
    loop(cols, codes_y)
    loop(16, codes_own)

    row_wait(1).wait_recv()
    received_to_turn(1)

    def state1_plane(x):
        cs[1, x] = turn_out(x).astype(BF)

    loop(slab_x, state1_plane, 2)
    send_col(3, cs.at[1], 0)
    col_wait(3).wait_recv()
    received_to_field(3, field1)

    def source1(c):
        for x in range(part_x):
            set_src_y(x, c, apply_y(field1, x, c))

    loop(cols, source1)

    def lines1(m):
        res = line_y_chunk(m, False).astype(BF)
        blocks = y_chunk // slab_y
        for b in range(blocks):
            for x in range(part_x):
                cs[2, (m * blocks + b) * part_x + x] = res[
                    b * slab_y:(b + 1) * slab_y, x * depth:(x + 1) * depth
                ]

    loop(total_y // y_chunk, lines1)
    send_col(4, cs.at[2], 0)

    row_wait(2).wait_recv()
    line_x_step(2, 3, True)
    send_row(3)

    col_wait(4).wait_recv()

    def state3_plane(x):
        source = apply_z(cr[4, x].astype(F32), cfz_s[x]).astype(BF)
        state3[1 + x] = dot_nt(source, lz[...]).astype(BF)

    loop(slab_x, state3_plane, 4)
    send_halo(2, state3)
    wait_halo(2, state3)

    def source3(x):
        turn_in(x, plane_x(state3, x))

    loop(slab_x, source3, 2)
    turned_to_send(4)
    send_row(4)

    row_wait(3).wait_recv()
    received_to_turn(3)

    def back3_plane(x):
        back3[1 + x] = turn_out(x).astype(BF)

    loop(slab_x, back3_plane, 2)
    send_halo(3, back3)
    wait_halo(3, back3)

    def face_sum(state, back, j):
        at_end = ((j == 0) & (row == 0)) | ((j == slab_x) & (row == rows - 1))
        keep = jnp.where(at_end, 0.0, 1.0).astype(F32)
        first = state[j + 1].astype(F32) - state[j].astype(F32)
        second = back[j + 1].astype(F32) - back[j].astype(F32)
        return keep * depth_sum(first * second)

    def faces_to_columns(state, back, keep_old):
        def one(j, before):
            here = face_sum(state, back, j + 1)
            total = here + before
            if keep_old:
                total = total + v_s[j]
            v_s[j] = total
            return here

        lax.fori_loop(0, slab_x, one, face_sum(state, back, 0), unroll=2)

    def adjoint3(x):
        source = plane_x(back3, x).astype(BF)
        backed = dot_nn(source, lz[...])
        state = cr[4, x].astype(F32)
        first = next_lane(state) - state
        second = next_lane(backed) - backed
        v_s[x] = 2.0 * depth_sum(first * second * lane_mask(state.shape))
        cs[3, x] = apply_z(backed, cfz_s[x]).astype(BF)

    loop(slab_x, adjoint3, 2)
    send_col(5, cs.at[3], 0)
    faces_to_columns(state3, back3, True)

    row_wait(4).wait_recv()
    line_x_step(4, 5, False)
    send_row(5)

    col_wait(5).wait_recv()

    def source_adj1(c):
        for x in range(part_x):
            set_src_y(x, c, cr[5, c * part_x + x])

    loop(cols, source_adj1)
    line_y_to_field(grad1, True)

    def adjoint1(c):
        for x in range(part_x):
            cs[4, c * part_x + x] = apply_y(grad1, x, c).astype(BF)

    loop(cols, adjoint1)
    send_col(6, cs.at[4], 0)

    def column_y1(c):
        for x in range(part_x):
            q_y[c * part_x + x] = grad_y(field1, grad1, x, c)

    loop(cols, column_y1)

    col_wait(6).wait_recv()

    def adjoint1_turn(x):
        turn_in(x, cr[6, x].astype(F32))

    loop(slab_x, adjoint1_turn, 2)
    turned_to_send(6)
    send_row(6)

    def zones_s(x):
        zone_add(v_s[x], zone_s_row(x), lo_s[x])

    loop(slab_x, zones_s)

    row_wait(5).wait_recv()
    received_to_turn(5)

    def state4_plane(x):
        cs[5, x] = turn_out(x).astype(BF)

    loop(slab_x, state4_plane, 2)
    send_col(7, cs.at[5], 0)
    col_wait(7).wait_recv()
    received_to_field(7, field4)

    def source4(c):
        for x in range(part_x):
            set_src_y(x, c, apply_y(field4, x, c))

    loop(cols, source4)

    row_wait(6).wait_recv()
    line_x_step(6, 7, True)
    send_row(7)

    def lines4(m):
        res = line_y_chunk(m, False).astype(BF).astype(F32)
        blocks = y_chunk // slab_y
        for b in range(blocks):
            for x in range(part_x):
                index = (m * blocks + b) * part_x + x
                state = res[b * slab_y:(b + 1) * slab_y, x * depth:(x + 1) * depth]
                backed = back5[index]
                first = next_lane(state) - state
                second = next_lane(backed) - backed
                v_y[index] = 2.0 * depth_sum(first * second * lane_mask(state.shape))

    loop(total_y // y_chunk, lines4)

    def column_y4(c):
        for x in range(part_x):
            q_y[c * part_x + x] = q_y[c * part_x + x] + grad_y(field4, grad4, x, c)

    loop(cols, column_y4)
    for x in range(part_x):
        line = jnp.concatenate([q_y[c * part_x + x] for c in range(cols)], axis=1)
        line = line + prev_lane(line)
        for c in range(cols):
            v_y[c * part_x + x] = v_y[c * part_x + x] + line[:, c * slab_y:(c + 1) * slab_y]

    def zones_y(c):
        for x in range(part_x):
            zone_add(v_y[c * part_x + x], zone_y_row(x, c), lo_y[c * part_x + x])

    loop(cols, zones_y)

    row_wait(7).wait_recv()
    received_to_turn(7)

    def back0_plane(x):
        back0[1 + x] = turn_out(x).astype(BF)

    loop(slab_x, back0_plane, 2)
    send_halo(4, back0)
    wait_halo(4, back0)
    faces_to_columns(head, back0, False)
    loop(slab_x, zones_s)

    sums = zacc[0:16, :] + zacc[16:32, :]
    high, low = split_two(sums * (-HALF_STEP * scale))
    parts = jnp.concatenate([high, low], axis=0)

    def to_owner(g):
        spread = dot_nn(parts, lo_own[g])
        spread = (spread[0:16] + spread[16:32]) * high_codes(owner[pl.ds(g, 1), :])
        z_send[g] = jnp.broadcast_to(jnp.sum(spread, axis=0, keepdims=True), (8, depth))

    loop(16, to_owner)

    def send_zone_row(i):
        r = row_peer(i + 1)
        pltpu.make_async_remote_copy(
            src_ref=z_send.at[r // 2], dst_ref=z_row.at[row],
            send_sem=zs_sem.at[0], recv_sem=zr_sem.at[0],
            device_id=(r, col), device_id_type=MESH,
        ).start()

    loop(rows - 1, send_zone_row)
    z_row[row] = z_send[row // 2]

    def last_plane(x):
        out_ref[x] = plane_x(back0, x).astype(BF)

    loop(slab_x, last_plane, 2)

    def zone_wait(phase, ref, count):
        part = pl.ds(0, count)
        return pltpu.make_async_remote_copy(
            src_ref=ref.at[part], dst_ref=ref.at[part],
            send_sem=zs_sem.at[phase], recv_sem=zr_sem.at[phase],
            device_id=(row, col), device_id_type=MESH,
        )

    zone_wait(0, z_row, rows - 1).wait_recv()
    z_mid[...] = jnp.sum(z_row[...], axis=0)

    def send_zone_col(i):
        c = col_peer(i + 1)
        pltpu.make_async_remote_copy(
            src_ref=z_mid, dst_ref=z_col.at[col],
            send_sem=zs_sem.at[1], recv_sem=zr_sem.at[1],
            device_id=(row, c), device_id_type=MESH,
        ).start()

    loop(cols - 1, send_zone_col)
    z_col[col] = z_mid[...]
    zone_wait(1, z_col, cols - 1).wait_recv()
    final = jnp.sum(z_col[...], axis=0)
    offset = lax.rem(row, 2) * (depth // 2) + col * 8
    zout_ref[...] = pltpu.roll(final, lax.rem(depth - offset, depth), axis=1)

    for k in range(8):
        row_wait(k).wait_send()
        col_wait(k).wait_send()
    for h, buf in enumerate((head, cond, state3, back3, back0)):
        for copy in halo_copies(h, buf):
            copy.wait_send()
    zone_wait(0, z_row, rows - 1).wait_send()
    zone_wait(1, z_col, cols - 1).wait_send()


def on_device(
    rows, cols, head_start, cotangent, conductivity, line_x, line_y, line_z, zone_map, owner_order
):
    slab_x, slab_y, depth = head_start.shape
    total_x, total_y = zone_map.shape
    zone_count = owner_order.shape[0]
    part_x = slab_x // cols
    part_y = slab_y // rows
    scale = 1.0 / math.sqrt(total_x * total_y * depth / zone_count)
    groups = zone_count // depth
    padded = pltpu.VMEM((slab_x + 2, slab_y, depth), BF)
    field = pltpu.VMEM((part_x, total_y + 2 * PAD, depth), F32)
    slab32 = pltpu.VMEM((slab_x, slab_y, depth), F32)
    sums = pltpu.VMEM((slab_x, 8, depth), F32)
    codes = pltpu.VMEM((16, depth, depth), BF)
    scratch = [
        padded, padded, padded, padded, padded,
        pltpu.VMEM((slab_x, slab_y, depth), BF),
        pltpu.VMEM(line_x.shape, BF),
        pltpu.VMEM(line_y.shape, BF),
        pltpu.VMEM(line_z.shape, BF),
        pltpu.VMEM((slab_x, slab_y), jnp.int32),
        pltpu.VMEM((8, total_y), jnp.int32),
        pltpu.VMEM((slab_x, slab_y), jnp.int32),
        pltpu.VMEM((groups, depth), jnp.int32),
        pltpu.VMEM((8, rows, part_y, slab_x, depth), BF),
        pltpu.VMEM((8, rows, part_y, slab_x, depth), BF),
        pltpu.VMEM((6, slab_x, slab_y, depth), BF),
        pltpu.VMEM((8, slab_x, slab_y, depth), BF),
        pltpu.VMEM((slab_x * slab_y, depth), F32),
        pltpu.VMEM((slab_x + 1, slab_y, depth), F32),
        slab32,
        field,
        slab32,
        field, field, field, field,
        slab32,
        pltpu.VMEM((total_y, part_x * depth), BF),
        sums, sums, sums,
        codes, codes, codes,
        pltpu.VMEM((32, depth), F32),
        pltpu.VMEM((groups, 8, depth), F32),
        pltpu.VMEM((8, depth), F32),
        pltpu.VMEM((rows, 8, depth), F32),
        pltpu.VMEM((cols, 8, depth), F32),
        pltpu.SemaphoreType.DMA((9,)),
        pltpu.SemaphoreType.DMA((8,)),
        pltpu.SemaphoreType.DMA((8,)),
        pltpu.SemaphoreType.DMA((8,)),
        pltpu.SemaphoreType.DMA((8,)),
        pltpu.SemaphoreType.DMA((5, 2)),
        pltpu.SemaphoreType.DMA((5, 2)),
        pltpu.SemaphoreType.DMA((2,)),
        pltpu.SemaphoreType.DMA((2,)),
    ]
    adjoint, zones = pl.pallas_call(
        functools.partial(kernel, rows, cols, scale),
        out_shape=(
            jax.ShapeDtypeStruct((slab_x, slab_y, depth), BF),
            jax.ShapeDtypeStruct((8, depth), F32),
        ),
        in_specs=[pl.BlockSpec(memory_space=pl.ANY)] * 8,
        out_specs=(
            pl.BlockSpec(memory_space=pltpu.VMEM),
            pl.BlockSpec(memory_space=pltpu.VMEM),
        ),
        scratch_shapes=scratch,
        compiler_params=pltpu.CompilerParams(
            collective_id=0, has_side_effects=True, vmem_limit_bytes=56 << 20
        ),
        name="adjoint_lines",
    )(
        head_start, cotangent, conductivity, line_x, line_y, line_z, zone_map,
        owner_order.reshape(groups, depth),
    )
    return adjoint, zones[0, : zone_count // (rows * cols)]


def solution(mesh):
    slab = P("row", "col", None)
    return jax.shard_map(
        functools.partial(on_device, mesh.shape["row"], mesh.shape["col"]),
        mesh=mesh,
        in_specs=(slab, slab, slab, P(), P(), P(), P(), P()),
        out_specs=(slab, P(("row", "col"))),
        check_vma=False,
    )
```

```python
import functools
import math

import jax
import jax.numpy as jnp
from jax import lax
from jax.experimental import pallas as pl
from jax.experimental.pallas import tpu as pltpu
from jax.sharding import PartitionSpec as P

MESH = pl.DeviceIdType.MESH
BF = jnp.bfloat16
F32 = jnp.float32
HALF_STEP = 0.075
PAD = 8


def dot_nn(a, b):
    return lax.dot_general(a, b, (((1,), (0,)), ((), ())), preferred_element_type=F32)


def dot_nt(a, b):
    return lax.dot_general(a, b, (((1,), (1,)), ((), ())), preferred_element_type=F32)


def dot_tn(a, b):
    return lax.dot_general(a, b, (((0,), (0,)), ((), ())), preferred_element_type=F32)


def loop(count, body, unroll=1):
    def step(i, carry):
        body(i)
        return carry

    lax.fori_loop(0, count, step, 0, unroll=unroll)


def split_two(values):
    high = values.astype(BF)
    low = (values - high.astype(F32)).astype(BF)
    return high, low


def kernel(
    rows, cols, scale,
    head_hbm, cot_hbm, cond_hbm, lx_hbm, ly_hbm, lz_hbm, zmap_hbm, owner_hbm,
    out_ref, zout_ref,
    head, cond, lx, ly, lz, zone_block, zone_turned, zone_y, owner,
    rs, rr, cs, cr, turn, cfx, cfy, cfz_y,
    field0, field3, grad3, grad0, field1, field4, grad4, grad1,
    back5, back2, state2, state5, src_x, src_y,
    zone_cols, zone_lines, lo_x, lo_y, lo_own, hi_own, spread_x, spread_y,
    zacc, z_send, z_mid, z_row, z_col,
    local_sem, rs_sem, rr_sem, cs_sem, cr_sem, zs_sem, zr_sem,
):
    row = lax.axis_index("row")
    col = lax.axis_index("col")
    slab_x, slab_y, depth = head_hbm.shape
    part_x = slab_x // cols
    total_x = lx.shape[0]
    total_y = ly.shape[0]
    half_y = slab_y // 2
    piece_y = half_y // rows

    def row_peer(i):
        return lax.rem(row + i, rows)

    def col_peer(i):
        return lax.rem(col + i, cols)

    loads = {}

    def load(slot, src, dst):
        copy = pltpu.make_async_copy(src, dst, local_sem.at[slot])
        copy.start()
        loads[slot] = copy

    own_x = pl.ds(col * part_x, part_x)
    load(0, cond_hbm, cond)
    load(1, head_hbm, head)
    load(2, cond_hbm.at[own_x], cr.at[0, own_x])
    load(3, cot_hbm.at[own_x], cr.at[1, own_x])
    load(4, lz_hbm, lz)
    load(5, lx_hbm, lx)
    load(6, ly_hbm, ly)
    load(7, zmap_hbm.at[:, pl.ds(pl.multiple_of(col * slab_y, slab_y), slab_y)], zone_block)
    load(8, zmap_hbm.at[pl.ds(row * slab_x + (col * part_x // 8) * 8, 8)], zone_y)
    load(9, owner_hbm, owner)

    barrier = pltpu.get_barrier_semaphore()

    def greet_row(i):
        pl.semaphore_signal(barrier, inc=1, device_id=(row_peer(i + 1), col), device_id_type=MESH)

    def greet_col(i):
        pl.semaphore_signal(barrier, inc=1, device_id=(row, col_peer(i + 1)), device_id_type=MESH)

    loop(rows - 1, greet_row)
    loop(cols - 1, greet_col)

    def near_last(k, count):
        return count // 2 + ((k + 1) // 2) * (1 - 2 * lax.rem(k, 2))

    ring_x = 4
    ring_z = rows // ring_x

    def send_row(k, h):
        def one(shift_z, shift_x):
            z = lax.rem(row // ring_x + shift_z, ring_z)
            x = lax.rem(lax.rem(row, ring_x) + shift_x, ring_x)
            r = z * ring_x + x
            pltpu.make_async_remote_copy(
                src_ref=rs.at[k, h, r], dst_ref=rr.at[k, h, row],
                send_sem=rs_sem.at[k, h], recv_sem=rr_sem.at[k, h],
                device_id=(r, col), device_id_type=MESH,
            ).start()

        shifts_z = [ring_z // 2 + ((i + 1) // 2) * (1 - 2 * (i % 2)) for i in range(ring_z)]

        def lines(i):
            for shift_z in shifts_z:
                one(shift_z, near_last(i, ring_x))

        loop(ring_x - 1, lines)
        for shift_z in shifts_z[:-1]:
            one(shift_z, 0)
        rr[k, h, row] = rs[k, h, row]

    def row_wait(k, h):
        part = pl.ds(0, rows - 1)
        return pltpu.make_async_remote_copy(
            src_ref=rs.at[k, h, part], dst_ref=rr.at[k, h, part],
            send_sem=rs_sem.at[k, h], recv_sem=rr_sem.at[k, h],
            device_id=(row, col), device_id_type=MESH,
        )

    all_y = pl.ds(0, slab_y)

    def half(h):
        return pl.ds(h * half_y, half_y)

    def send_col(j, slot, src, ys):
        def one(i):
            c = col_peer(i + 1)
            pltpu.make_async_remote_copy(
                src_ref=src.at[pl.ds(c * part_x, part_x), ys],
                dst_ref=cr.at[j, own_x, ys],
                send_sem=cs_sem.at[j, slot], recv_sem=cr_sem.at[j, slot],
                device_id=(row, c), device_id_type=MESH,
            ).start()

        loop(cols - 1, one)

    def keep_own(j, src, ys):
        cr[j, own_x, ys] = src[own_x, ys]

    def col_wait(j, slot, ys):
        part = pl.ds(0, (cols - 1) * part_x)
        return pltpu.make_async_remote_copy(
            src_ref=cr.at[j, part, ys], dst_ref=cr.at[j, part, ys],
            send_sem=cs_sem.at[j, slot], recv_sem=cr_sem.at[j, slot],
            device_id=(row, col), device_id_type=MESH,
        )

    def next_lane(f):
        return pltpu.roll(f, f.shape[1] - 1, axis=1)

    def prev_lane(f):
        return pltpu.roll(f, 1, axis=1)

    def apply_z(f, faces):
        flux = faces * (next_lane(f) - f)
        return f + flux - prev_lane(flux)

    def lane_mask(shape):
        lane = lax.broadcasted_iota(jnp.int32, shape, 1)
        return jnp.where(lane < depth - 1, 1.0, 0.0).astype(F32)

    ones8 = jnp.ones((8, 2 * depth), BF)

    def depth_sum(products):
        high, low = split_two(products)
        return dot_nt(ones8, jnp.concatenate([high, low], axis=1))

    def turn_in(x, h, plane):
        turn[pl.ds(h * half_y * slab_x + x, half_y, stride=slab_x), :] = plane

    def turn_out(x, h):
        return turn[pl.ds(h * half_y * slab_x + x, half_y, stride=slab_x), :]

    group = 4
    block = group * piece_y * slab_x

    def turned_to_send(k, h):
        def one(g):
            base = pl.multiple_of(h * half_y * slab_x + g * block, block)
            piece = turn[pl.ds(base, block), :].astype(BF)
            rs[k, h, pl.ds(g * group, group)] = piece.reshape(group, piece_y, slab_x, depth)

        loop(rows // group, one, 2)

    def received_to_turn(k, h):
        def one(g):
            base = pl.multiple_of(h * half_y * slab_x + g * block, block)
            piece = rr[k, h, pl.ds(g * group, group)].reshape(block, depth)
            turn[pl.ds(base, block), :] = piece.astype(F32)

        loop(rows // group, one, 2)

    def received_to_planes(k, h, buf, offset):
        received_to_turn(k, h)

        def one(x):
            buf[offset + x, half(h)] = turn_out(x, h).astype(BF)

        loop(slab_x, one, 4)

    def hub_planes_to_send(buf, k):
        def one(x):
            for h in range(2):
                turn_in(x, h, buf[x, half(h)].astype(F32))

        loop(slab_x, one, 2)
        turned_to_send(k, 0)
        turned_to_send(k, 1)

    def hub_to_lines(k, j, h):
        buf = cs.at[j]
        received_to_planes(k, h, buf, 0)
        send_col(j, h, buf, half(h))
        keep_own(j, buf, half(h))

    chunk = 128
    peers_chunk = chunk // slab_x
    chunks_x = total_x // chunk

    def received_x(k, h, y, c):
        return rr[k, h, pl.ds(c * peers_chunk, peers_chunk), y].reshape(chunk, depth)

    def to_send_x(k, h, y, c, values):
        rs[k, h, pl.ds(c * peers_chunk, peers_chunk), y] = values.astype(BF).reshape(
            peers_chunk, slab_x, depth
        )

    def rows_of(c):
        return pl.ds(pl.multiple_of(PAD + c * chunk, 8), chunk)

    def each_x(body, unroll=1):
        def one(c):
            for y in range(piece_y):
                body(y, c)

        loop(chunks_x, one, unroll)

    def pad_lines_x(field, h):
        for y in range(piece_y):
            pad_line(field, h * piece_y + y, total_x)

    def received_to_field_x(k, h, field):
        def one(y, c):
            field[h * piece_y + y, rows_of(c), :] = received_x(k, h, y, c).astype(F32)

        each_x(one)
        pad_lines_x(field, h)

    def src_part(c):
        return pl.ds(pl.multiple_of(c * chunk, chunk), chunk)

    def forward_x(k_in, k_out, h, field):
        received_to_field_x(k_in, h, field)

        def source(y, c):
            src_x[src_part(c), y * depth:(y + 1) * depth] = apply_lines(
                field, cfx, h * piece_y + y, c
            ).astype(BF)

        each_x(source)

        def line(c):
            res = dot_nn(lx[src_part(c), :], src_x[...])
            for y in range(piece_y):
                to_send_x(k_out, h, y, c, res[:, y * depth:(y + 1) * depth])

        loop(chunks_x, line, 2)
        send_row(k_out, h)

    def adjoint_x(k_in, k_out, h, grad):
        rhs = jnp.concatenate(
            [rr[k_in, h, :, y].reshape(total_x, depth) for y in range(piece_y)], axis=1
        )

        def line(c):
            res = dot_tn(lx[:, src_part(c)], rhs)
            for y in range(piece_y):
                grad[h * piece_y + y, rows_of(c), :] = res[:, y * depth:(y + 1) * depth]

        loop(chunks_x, line, 2)
        pad_lines_x(grad, h)

        def flux(y, c):
            to_send_x(k_out, h, y, c, apply_lines(grad, cfx, h * piece_y + y, c))

        each_x(flux)
        send_row(k_out, h)

    y_chunk = 256
    blocks = y_chunk // slab_y

    def line_y_chunk(m, transpose):
        part = pl.ds(pl.multiple_of(m * y_chunk, y_chunk), y_chunk)
        if transpose:
            return dot_tn(ly[:, part], src_y[...])
        return dot_nn(ly[part, :], src_y[...])

    def line_y_to_field(field):
        def one(m):
            res = line_y_chunk(m, True)
            for x in range(part_x):
                field[x, pl.ds(pl.multiple_of(PAD + m * y_chunk, 8), y_chunk), :] = res[
                    :, x * depth:(x + 1) * depth
                ]

        loop(total_y // y_chunk, one)
        pad_field(field)

    def line_y_to_blocks(body):
        def one(m):
            res = line_y_chunk(m, False).astype(BF)
            for b in range(blocks):
                for x in range(part_x):
                    body(
                        (m * blocks + b) * part_x + x,
                        res[b * slab_y:(b + 1) * slab_y, x * depth:(x + 1) * depth],
                    )

        loop(total_y // y_chunk, one)

    def pad_line(field, line, length):
        field[line, 0:PAD, :] = jnp.broadcast_to(field[line, PAD:PAD + 1, :], (PAD, depth))
        field[line, PAD + length:, :] = jnp.broadcast_to(
            field[line, PAD + length - 1:PAD + length, :], (PAD, depth)
        )

    def pad_field(field):
        for x in range(part_x):
            pad_line(field, x, total_y)

    def received_to_field(j, field):
        def one(c):
            for x in range(part_x):
                field[x, pl.ds(pl.multiple_of(PAD + c * slab_y, 8), slab_y), :] = cr[
                    j, c * part_x + x
                ].astype(F32)

        loop(cols, one, 2)
        pad_field(field)

    def three(field, x, c):
        base = pl.multiple_of(PAD + c * slab_y, 8)
        return (
            field[x, pl.ds(base - 1, slab_y), :],
            field[x, pl.ds(base, slab_y), :],
            field[x, pl.ds(base + 1, slab_y), :],
        )

    def apply_lines(field, faces, x, c):
        below, mid, above = three(field, x, c)
        face_below, face, _ = three(faces, x, c)
        return mid + face * (above - mid) - face_below * (mid - below)

    def apply_y(field, x, c):
        return apply_lines(field, cfy, x, c)

    def cells_line(field, grad, x, c):
        below, mid, above = three(field, x, c)
        g_below, g_mid, g_above = three(grad, x, c)
        return (above - mid) * (g_above - g_mid) + (mid - below) * (g_mid - g_below)

    def faces_line(field, faces, x, c):
        _, mid, above = three(field, x, c)
        faces[x, rows_of(c), :] = HALF_STEP * (mid + above)

    def close_faces(faces, x, length):
        faces[x, 0:PAD, :] = jnp.zeros((PAD, depth), F32)
        faces[x, PAD + length - 1:PAD + length, :] = jnp.zeros((1, depth), F32)
        faces[x, PAD + length:, :] = jnp.zeros((PAD, depth), F32)

    def cells_z(state, backed):
        first = next_lane(state) - state
        second = next_lane(backed) - backed
        return 2.0 * first * second * lane_mask(state.shape)

    def set_src_y(x, c, values):
        src_y[pl.ds(pl.multiple_of(c * slab_y, slab_y), slab_y), x * depth:(x + 1) * depth] = (
            values.astype(BF)
        )

    def source_y(field):
        def one(c):
            for x in range(part_x):
                set_src_y(x, c, apply_y(field, x, c))

        loop(cols, one)

    def low_codes(zones):
        code = jnp.broadcast_to(zones & (depth - 1), (depth, depth))
        return jnp.where(
            code == lax.broadcasted_iota(jnp.int32, (depth, depth), 0), 1.0, 0.0
        ).astype(BF)

    def high_codes(zones):
        code = jnp.broadcast_to(zones // depth, (16, depth))
        return jnp.where(code == lax.broadcasted_iota(jnp.int32, (16, depth), 0), 1.0, 0.0)

    def spread(sums, zones):
        both = jnp.concatenate([sums, sums], axis=0) * high_codes(zones)
        high, low = split_two(both)
        return jnp.concatenate([high, low], axis=0)

    def lanes(index):
        return pl.ds(pl.multiple_of(index * depth, depth), depth)

    def set_codes():
        groups = 8 // part_x
        for x in range(part_x):
            line = jnp.zeros((1, total_y), jnp.int32)
            for g in range(groups):
                mine = jnp.where(lax.rem(col, groups) == g, 1, 0)
                line = line + mine * zone_y[g * part_x + x:g * part_x + x + 1, :]
            for c in range(cols):
                index = c * part_x + x
                zone_lines[index:index + 1, :] = line[:, c * slab_y:(c + 1) * slab_y]
        for c in range(chunks_x):
            block = zone_block[c * chunk:(c + 1) * chunk, :].astype(F32)
            zone_turned[c] = jnp.transpose(block)
        for h in range(2):
            for y in range(piece_y):
                for c in range(chunks_x):
                    index = (h * piece_y + y) * chunks_x + c
                    place = pl.ds(h * half_y + row * piece_y + y, 1)
                    zone_cols[index:index + 1, :] = zone_turned[c, place, :].astype(jnp.int32)

        def one(i):
            lo_x[:, lanes(i)] = low_codes(zone_cols[pl.ds(i, 1), :])
            lo_y[:, lanes(i)] = low_codes(zone_lines[pl.ds(i, 1), :])
            own = owner[pl.ds(i, 1), :]
            lo_own[:, lanes(i)] = low_codes(own)
            hi_own[:, lanes(i)] = high_codes(own)

        loop(16, one)

    def zones_x(field, grad, h):
        def one(c):
            for y in range(piece_y):
                line = h * piece_y + y
                index = line * chunks_x + c
                spread_x[:, lanes(index)] = spread(
                    depth_sum(cells_line(field, grad, line, c)), zone_cols[pl.ds(index, 1), :]
                )

        loop(chunks_x, one, 2)
        count = piece_y * chunks_x * depth
        part = slice(h * count, (h + 1) * count)
        zacc[...] += dot_nt(spread_x[:, part], lo_x[:, part])

    def zones_y():
        def one(c):
            for x in range(part_x):
                index = c * part_x + x
                cells = cells_line(field1, grad1, x, c) + cells_line(field4, grad4, x, c)
                cells = cells + cells_z(state2[index].astype(F32), back2[index])
                cells = cells + cells_z(state5[index].astype(F32), back5[index])
                spread_y[:, lanes(index)] = spread(
                    depth_sum(cells), zone_lines[pl.ds(index, 1), :]
                )

        loop(cols, one)
        zacc[...] += dot_nt(spread_y[...], lo_y[...])

    def back_z(j, back):
        def one(c):
            for x in range(part_x):
                index = c * part_x + x
                backed = dot_nn(cr[j, index], lz[...])
                back[index] = backed
                set_src_y(x, c, apply_z(backed, cfz_y[index]))

        loop(cols, one, 2)

    def back_y(j, grad):
        line_y_to_field(grad)

        def one(c):
            for x in range(part_x):
                cs[j, c * part_x + x] = apply_y(grad, x, c).astype(BF)

        loop(cols, one)
        send_col(j, 0, cs.at[j], all_y)
        keep_own(j, cs.at[j], all_y)

    loads[0].wait()
    hub_planes_to_send(cond, 0)
    loads[1].wait()
    hub_planes_to_send(head, 1)
    pl.semaphore_wait(barrier, rows + cols - 2)
    send_col(1, 0, cot_hbm, all_y)
    send_col(0, 0, cond_hbm, all_y)
    for h in range(2):
        send_row(0, h)
        send_row(1, h)

    for slot in (2, 3, 4, 5, 6):
        loads[slot].wait()
    col_wait(0, 0, all_y).wait_recv()
    received_to_field(0, field1)

    def faces_y(c):
        for x in range(part_x):
            index = c * part_x + x
            own = cr[0, index].astype(F32)
            cfz_y[index] = HALF_STEP * (own + next_lane(own)) * lane_mask(own.shape)
            faces_line(field1, cfy, x, c)

    loop(cols, faces_y)
    for x in range(part_x):
        close_faces(cfy, x, total_y)
    col_wait(1, 0, all_y).wait_recv()
    back_z(1, back5)
    back_y(2, grad4)

    zacc[...] = jnp.zeros(zacc.shape, F32)
    for h in range(2):
        row_wait(0, h).wait_recv()
        received_to_field_x(0, h, field3)

        def faces_x(y, c):
            faces_line(field3, cfx, h * piece_y + y, c)

        each_x(faces_x)
        for y in range(piece_y):
            close_faces(cfx, h * piece_y + y, total_x)
        row_wait(1, h).wait_recv()
        forward_x(1, 2, h, field0)
    for slot in (7, 8, 9):
        loads[slot].wait()
    set_codes()

    col_wait(2, 0, all_y).wait_recv()
    hub_planes_to_send(cr.at[2], 3)
    for h in range(2):
        row_wait(2, h).wait_recv()
        send_row(3, h)
        hub_to_lines(2, 3, h)

    row_wait(3, 0).wait_recv()
    adjoint_x(3, 4, 0, grad3)

    for h in range(2):
        col_wait(3, h, half(h)).wait_recv()
    received_to_field(3, field1)
    source_y(field1)

    def state3_block(index, state):
        state2[index] = state
        source = apply_z(state.astype(F32), cfz_y[index]).astype(BF)
        cs[4, index] = dot_nt(source, lz[...]).astype(BF)

    line_y_to_blocks(state3_block)
    send_col(4, 0, cs.at[4], all_y)
    keep_own(4, cs.at[4], all_y)

    row_wait(3, 1).wait_recv()
    adjoint_x(3, 4, 1, grad3)
    col_wait(4, 0, all_y).wait_recv()
    hub_planes_to_send(cr.at[4], 5)

    for h in range(2):
        row_wait(4, h).wait_recv()
        send_row(5, h)
        hub_to_lines(4, 5, h)

    row_wait(5, 0).wait_recv()
    forward_x(5, 6, 0, field3)

    for h in range(2):
        col_wait(5, h, half(h)).wait_recv()
    back_z(5, back2)
    back_y(6, grad1)

    row_wait(5, 1).wait_recv()
    forward_x(5, 6, 1, field3)
    zones_x(field3, grad3, 0)
    zones_x(field3, grad3, 1)
    col_wait(6, 0, all_y).wait_recv()
    hub_planes_to_send(cr.at[6], 7)

    for h in range(2):
        row_wait(6, h).wait_recv()
        send_row(7, h)
        hub_to_lines(6, 7, h)

    row_wait(7, 0).wait_recv()
    adjoint_x(7, 8, 0, grad0)

    for h in range(2):
        col_wait(7, h, half(h)).wait_recv()
    received_to_field(7, field4)
    source_y(field4)

    def state5_block(index, state):
        state5[index] = state

    line_y_to_blocks(state5_block)
    zones_y()
    zones_x(field0, grad0, 0)

    row_wait(7, 1).wait_recv()
    adjoint_x(7, 8, 1, grad0)
    zones_x(field0, grad0, 1)

    sums = (zacc[0:16, :] + zacc[16:32, :]) * (-HALF_STEP * scale)
    high, low = split_two(sums)
    ordered = dot_nn(jnp.concatenate([high, low], axis=0), lo_own[...])
    ordered = (ordered[0:16] + ordered[16:32]) * hi_own[...]
    ordered = jnp.sum(ordered, axis=0, keepdims=True)
    for g in range(z_send.shape[0]):
        z_send[g] = jnp.broadcast_to(ordered[:, g * depth:(g + 1) * depth], (8, depth))

    def send_zone_row(i):
        r = row_peer(i + 1)
        pltpu.make_async_remote_copy(
            src_ref=z_send.at[r // 2], dst_ref=z_row.at[row],
            send_sem=zs_sem.at[0], recv_sem=zr_sem.at[0],
            device_id=(r, col), device_id_type=MESH,
        ).start()

    loop(rows - 1, send_zone_row)
    z_row[row] = z_send[row // 2]
    row_wait(8, 0).wait_recv()
    received_to_planes(8, 0, out_ref, 0)

    def zone_wait(phase, ref, count):
        part = pl.ds(0, count)
        return pltpu.make_async_remote_copy(
            src_ref=ref.at[part], dst_ref=ref.at[part],
            send_sem=zs_sem.at[phase], recv_sem=zr_sem.at[phase],
            device_id=(row, col), device_id_type=MESH,
        )

    zone_wait(0, z_row, rows - 1).wait_recv()
    z_mid[...] = jnp.sum(z_row[...], axis=0)

    def send_zone_col(i):
        c = col_peer(i + 1)
        pltpu.make_async_remote_copy(
            src_ref=z_mid, dst_ref=z_col.at[col],
            send_sem=zs_sem.at[1], recv_sem=zr_sem.at[1],
            device_id=(row, c), device_id_type=MESH,
        ).start()

    loop(cols - 1, send_zone_col)
    z_col[col] = z_mid[...]
    row_wait(8, 1).wait_recv()
    received_to_planes(8, 1, out_ref, 0)
    zone_wait(1, z_col, cols - 1).wait_recv()
    final = jnp.sum(z_col[...], axis=0)
    offset = lax.rem(row, 2) * (depth // 2) + col * 8
    zout_ref[...] = pltpu.roll(final, lax.rem(depth - offset, depth), axis=1)

    for k in range(9):
        for h in range(2):
            row_wait(k, h).wait_send()
    for j in (0, 1, 2, 4, 6):
        col_wait(j, 0, all_y).wait_send()
    for j in (3, 5, 7):
        for h in range(2):
            col_wait(j, h, half(h)).wait_send()
    zone_wait(0, z_row, rows - 1).wait_send()
    zone_wait(1, z_col, cols - 1).wait_send()


def on_device(
    rows, cols, head_start, cotangent, conductivity, line_x, line_y, line_z, zone_map, owner_order
):
    slab_x, slab_y, depth = head_start.shape
    total_x, total_y = zone_map.shape
    zone_count = owner_order.shape[0]
    part_x = slab_x // cols
    part_y = slab_y // rows
    scale = 1.0 / math.sqrt(total_x * total_y * depth / zone_count)
    groups = zone_count // depth
    lines_x = pltpu.VMEM((part_y, total_x + 2 * PAD, depth), F32)
    lines_y = pltpu.VMEM((part_x, total_y + 2 * PAD, depth), F32)
    slab16 = pltpu.VMEM((slab_x, slab_y, depth), BF)
    slab32 = pltpu.VMEM((slab_x, slab_y, depth), F32)
    codes = pltpu.VMEM((depth, slab_x * slab_y), BF)
    spread = pltpu.VMEM((32, slab_x * slab_y), BF)
    row_slots = pltpu.VMEM((9, 2, rows, part_y // 2, slab_x, depth), BF)
    col_slots = pltpu.VMEM((8, slab_x, slab_y, depth), BF)
    scratch = [
        slab16, slab16,
        pltpu.VMEM(line_x.shape, BF),
        pltpu.VMEM(line_y.shape, BF),
        pltpu.VMEM(line_z.shape, BF),
        pltpu.VMEM((total_x, slab_y), jnp.int32),
        pltpu.VMEM((total_x // 128, slab_y, 128), F32),
        pltpu.VMEM((8, total_y), jnp.int32),
        pltpu.VMEM((groups, depth), jnp.int32),
        row_slots, row_slots, col_slots, col_slots,
        pltpu.VMEM((slab_x * slab_y, depth), F32),
        lines_x, lines_y, slab32,
        lines_x, lines_x, lines_x, lines_x,
        lines_y, lines_y, lines_y, lines_y,
        slab32, slab32, slab16, slab16,
        pltpu.VMEM((total_x, part_y // 2 * depth), BF),
        pltpu.VMEM((total_y, part_x * depth), BF),
        pltpu.VMEM((16, depth), jnp.int32),
        pltpu.VMEM((16, depth), jnp.int32),
        codes, codes, codes,
        pltpu.VMEM((16, zone_count), F32),
        spread, spread,
        pltpu.VMEM((32, depth), F32),
        pltpu.VMEM((groups, 8, depth), F32),
        pltpu.VMEM((8, depth), F32),
        pltpu.VMEM((rows, 8, depth), F32),
        pltpu.VMEM((cols, 8, depth), F32),
        pltpu.SemaphoreType.DMA((10,)),
        pltpu.SemaphoreType.DMA((9, 2)),
        pltpu.SemaphoreType.DMA((9, 2)),
        pltpu.SemaphoreType.DMA((8, 2)),
        pltpu.SemaphoreType.DMA((8, 2)),
        pltpu.SemaphoreType.DMA((2,)),
        pltpu.SemaphoreType.DMA((2,)),
    ]
    adjoint, zones = pl.pallas_call(
        functools.partial(kernel, rows, cols, scale),
        out_shape=(
            jax.ShapeDtypeStruct((slab_x, slab_y, depth), BF),
            jax.ShapeDtypeStruct((8, depth), F32),
        ),
        in_specs=[pl.BlockSpec(memory_space=pl.ANY)] * 8,
        out_specs=(
            pl.BlockSpec(memory_space=pltpu.VMEM),
            pl.BlockSpec(memory_space=pltpu.VMEM),
        ),
        scratch_shapes=scratch,
        compiler_params=pltpu.CompilerParams(
            collective_id=0, has_side_effects=True, vmem_limit_bytes=56 << 20
        ),
        name="adjoint_lines",
    )(
        head_start, cotangent, conductivity, line_x, line_y, line_z, zone_map,
        owner_order.reshape(groups, depth),
    )
    return adjoint, zones[0, : zone_count // (rows * cols)]


def solution(mesh):
    slab = P("row", "col", None)
    return jax.shard_map(
        functools.partial(on_device, mesh.shape["row"], mesh.shape["col"]),
        mesh=mesh,
        in_specs=(slab, slab, slab, P(), P(), P(), P(), P()),
        out_specs=(slab, P(("row", "col"))),
        check_vma=False,
    )
```

```python
import functools
import math

import jax
import jax.numpy as jnp
from jax import lax
from jax.experimental import pallas as pl
from jax.experimental.pallas import tpu as pltpu
from jax.sharding import PartitionSpec as P

MESH = pl.DeviceIdType.MESH
BF = jnp.bfloat16
F32 = jnp.float32
HALF_STEP = 0.075
PAD = 8


def dot_nn(a, b):
    return lax.dot_general(a, b, (((1,), (0,)), ((), ())), preferred_element_type=F32)


def dot_nt(a, b):
    return lax.dot_general(a, b, (((1,), (1,)), ((), ())), preferred_element_type=F32)


def dot_tn(a, b):
    return lax.dot_general(a, b, (((0,), (0,)), ((), ())), preferred_element_type=F32)


def loop(count, body, unroll=1):
    def step(i, carry):
        body(i)
        return carry

    lax.fori_loop(0, count, step, 0, unroll=unroll)


def split_two(values):
    high = values.astype(BF)
    low = (values - high.astype(F32)).astype(BF)
    return high, low


def kernel(
    rows, cols, scale,
    head_hbm, cot_hbm, cond_hbm, lx_hbm, ly_hbm, lz_hbm, zmap_hbm, owner_hbm,
    out_ref, zout_ref,
    head, cond, lx, ly, lz, zone_block, zone_turned, zone_y, owner,
    rs, rr, cs, cr, turn, cfx, cfy, cfz_y,
    field0, field3, grad3, grad0, field1, field4, grad4, grad1,
    back5, back2, state2, state5, src_x, src_y,
    zone_cols, zone_lines, lo_x, lo_y, lo_own, hi_own, spread_x, spread_y,
    zacc, z_send, z_mid, z_row, z_col,
    local_sem, rs_sem, rr_sem, cs_sem, cr_sem, zs_sem, zr_sem,
):
    row = lax.axis_index("row")
    col = lax.axis_index("col")
    slab_x, slab_y, depth = head_hbm.shape
    part_x = slab_x // cols
    total_x = lx.shape[0]
    total_y = ly.shape[0]
    half_y = slab_y // 2
    piece_y = half_y // rows

    def row_peer(i):
        return lax.rem(row + i, rows)

    def col_peer(i):
        return lax.rem(col + i, cols)

    loads = {}

    def load(slot, src, dst):
        copy = pltpu.make_async_copy(src, dst, local_sem.at[slot])
        copy.start()
        loads[slot] = copy

    own_x = pl.ds(col * part_x, part_x)
    load(0, cond_hbm, cond)
    load(1, head_hbm, head)

    barrier = pltpu.get_barrier_semaphore()

    def greet_row(i):
        pl.semaphore_signal(barrier, inc=1, device_id=(row_peer(i + 1), col), device_id_type=MESH)

    def greet_col(i):
        pl.semaphore_signal(barrier, inc=1, device_id=(row, col_peer(i + 1)), device_id_type=MESH)

    loop(rows - 1, greet_row)
    loop(cols - 1, greet_col)
    load(2, cond_hbm.at[own_x], cr.at[0, own_x])
    load(3, cot_hbm.at[own_x], cr.at[1, own_x])
    load(4, lz_hbm, lz)
    load(5, lx_hbm, lx)
    load(6, ly_hbm, ly)
    load(7, zmap_hbm.at[:, pl.ds(pl.multiple_of(col * slab_y, slab_y), slab_y)], zone_block)
    load(8, zmap_hbm.at[pl.ds(row * slab_x + (col * part_x // 8) * 8, 8)], zone_y)
    load(9, owner_hbm, owner)

    def near_last(k, count):
        return count // 2 + ((k + 1) // 2) * (1 - 2 * lax.rem(k, 2))

    ring_x = 4
    side = lax.rem(col, 2)
    ring_z = rows // ring_x

    def send_row(k, h):
        def one(shift_z, shift_x):
            z = lax.rem(row // ring_x + shift_z + side * (ring_z - 2 * shift_z), ring_z)
            x = lax.rem(lax.rem(row, ring_x) + shift_x + side * (ring_x - 2 * shift_x), ring_x)
            r = z * ring_x + x
            pltpu.make_async_remote_copy(
                src_ref=rs.at[k, h, r], dst_ref=rr.at[k, h, row],
                send_sem=rs_sem.at[k, h], recv_sem=rr_sem.at[k, h],
                device_id=(r, col), device_id_type=MESH,
            ).start()

        shifts_z = [ring_z // 2 + ((i + 1) // 2) * (1 - 2 * (i % 2)) for i in range(ring_z)]

        def lines(i):
            for shift_z in shifts_z:
                one(shift_z, near_last(i, ring_x))

        loop(ring_x - 1, lines)
        for shift_z in shifts_z[:-1]:
            one(shift_z, 0)
        rr[k, h, row] = rs[k, h, row]

    def row_wait(k, h):
        part = pl.ds(0, rows - 1)
        return pltpu.make_async_remote_copy(
            src_ref=rs.at[k, h, part], dst_ref=rr.at[k, h, part],
            send_sem=rs_sem.at[k, h], recv_sem=rr_sem.at[k, h],
            device_id=(row, col), device_id_type=MESH,
        )

    all_y = pl.ds(0, slab_y)

    def half(h):
        return pl.ds(h * half_y, half_y)

    def send_col(j, slot, src, ys):
        def one(i):
            c = col_peer(i + 1)
            pltpu.make_async_remote_copy(
                src_ref=src.at[pl.ds(c * part_x, part_x), ys],
                dst_ref=cr.at[j, own_x, ys],
                send_sem=cs_sem.at[j, slot], recv_sem=cr_sem.at[j, slot],
                device_id=(row, c), device_id_type=MESH,
            ).start()

        loop(cols - 1, one)

    def keep_own(j, src, ys):
        cr[j, own_x, ys] = src[own_x, ys]

    def col_wait(j, slot, ys):
        part = pl.ds(0, (cols - 1) * part_x)
        return pltpu.make_async_remote_copy(
            src_ref=cr.at[j, part, ys], dst_ref=cr.at[j, part, ys],
            send_sem=cs_sem.at[j, slot], recv_sem=cr_sem.at[j, slot],
            device_id=(row, col), device_id_type=MESH,
        )

    def next_lane(f):
        return pltpu.roll(f, f.shape[1] - 1, axis=1)

    def prev_lane(f):
        return pltpu.roll(f, 1, axis=1)

    def apply_z(f, faces):
        flux = faces * (next_lane(f) - f)
        return f + flux - prev_lane(flux)

    def lane_mask(shape):
        lane = lax.broadcasted_iota(jnp.int32, shape, 1)
        return jnp.where(lane < depth - 1, 1.0, 0.0).astype(F32)

    ones8 = jnp.ones((8, 2 * depth), BF)

    def depth_sum(products):
        high, low = split_two(products)
        return dot_nt(ones8, jnp.concatenate([high, low], axis=1))

    def turn_in(x, h, plane):
        turn[pl.ds(h * half_y * slab_x + x, half_y, stride=slab_x), :] = plane

    def turn_out(x, h):
        return turn[pl.ds(h * half_y * slab_x + x, half_y, stride=slab_x), :]

    group = 4
    block = group * piece_y * slab_x

    def turned_to_send(k, h):
        def one(g):
            base = pl.multiple_of(h * half_y * slab_x + g * block, block)
            piece = turn[pl.ds(base, block), :].astype(BF)
            rs[k, h, pl.ds(g * group, group)] = piece.reshape(group, piece_y, slab_x, depth)

        loop(rows // group, one, 2)

    def received_to_turn(k, h):
        def one(g):
            base = pl.multiple_of(h * half_y * slab_x + g * block, block)
            piece = rr[k, h, pl.ds(g * group, group)].reshape(block, depth)
            turn[pl.ds(base, block), :] = piece.astype(F32)

        loop(rows // group, one, 2)

    def received_to_planes(k, h, buf, offset):
        received_to_turn(k, h)

        def one(x):
            buf[offset + x, half(h)] = turn_out(x, h).astype(BF)

        loop(slab_x, one, 4)

    def half_planes_to_send(buf, k, h):
        def one(x):
            turn_in(x, h, buf[x, half(h)].astype(F32))

        loop(slab_x, one, 4)
        turned_to_send(k, h)

    def hub_planes_to_send(buf, k):
        for h in range(2):
            half_planes_to_send(buf, k, h)

    def hub_to_lines(k, j, h):
        buf = cs.at[j]
        received_to_planes(k, h, buf, 0)
        send_col(j, h, buf, half(h))
        keep_own(j, buf, half(h))

    chunk = 128
    peers_chunk = chunk // slab_x
    chunks_x = total_x // chunk

    def received_x(k, h, y, c):
        return rr[k, h, pl.ds(c * peers_chunk, peers_chunk), y].reshape(chunk, depth)

    def to_send_x(k, h, y, c, values):
        rs[k, h, pl.ds(c * peers_chunk, peers_chunk), y] = values.astype(BF).reshape(
            peers_chunk, slab_x, depth
        )

    def rows_of(c):
        return pl.ds(pl.multiple_of(PAD + c * chunk, 8), chunk)

    def each_x(body, unroll=1):
        def one(c):
            for y in range(piece_y):
                body(y, c)

        loop(chunks_x, one, unroll)

    def pad_lines_x(field, h):
        for y in range(piece_y):
            pad_line(field, h * piece_y + y, total_x)

    def received_to_field_x(k, h, field):
        def one(y, c):
            field[h * piece_y + y, rows_of(c), :] = received_x(k, h, y, c).astype(F32)

        each_x(one)
        pad_lines_x(field, h)

    def src_part(c):
        return pl.ds(pl.multiple_of(c * chunk, chunk), chunk)

    def forward_x(k_in, k_out, h, field):
        received_to_field_x(k_in, h, field)

        def source(y, c):
            src_x[src_part(c), y * depth:(y + 1) * depth] = apply_lines(
                field, cfx, h * piece_y + y, c
            ).astype(BF)

        each_x(source)

        def line(c):
            res = dot_nn(lx[src_part(c), :], src_x[...])
            for y in range(piece_y):
                to_send_x(k_out, h, y, c, res[:, y * depth:(y + 1) * depth])

        loop(chunks_x, line, 2)
        send_row(k_out, h)

    def back_x(k_in, h, grad):
        rhs = jnp.concatenate(
            [rr[k_in, h, :, y].reshape(total_x, depth) for y in range(piece_y)], axis=1
        )

        def line(c):
            res = dot_tn(lx[:, src_part(c)], rhs)
            for y in range(piece_y):
                grad[h * piece_y + y, rows_of(c), :] = res[:, y * depth:(y + 1) * depth]

        loop(chunks_x, line, 2)
        pad_lines_x(grad, h)

    def flux_x(k_out, h, grad):
        def flux(y, c):
            to_send_x(k_out, h, y, c, apply_lines(grad, cfx, h * piece_y + y, c))

        each_x(flux)
        send_row(k_out, h)

    def adjoint_x(k_in, k_out, h, grad):
        back_x(k_in, h, grad)
        flux_x(k_out, h, grad)

    y_chunk = 256
    blocks = y_chunk // slab_y

    def line_y_chunk(m, transpose):
        part = pl.ds(pl.multiple_of(m * y_chunk, y_chunk), y_chunk)
        if transpose:
            return dot_tn(ly[:, part], src_y[...])
        return dot_nn(ly[part, :], src_y[...])

    def line_y_to_field(field):
        def one(m):
            res = line_y_chunk(m, True)
            for x in range(part_x):
                field[x, pl.ds(pl.multiple_of(PAD + m * y_chunk, 8), y_chunk), :] = res[
                    :, x * depth:(x + 1) * depth
                ]

        loop(total_y // y_chunk, one)
        pad_field(field)

    def line_y_to_blocks(body):
        def one(m):
            res = line_y_chunk(m, False).astype(BF)
            for b in range(blocks):
                for x in range(part_x):
                    body(
                        (m * blocks + b) * part_x + x,
                        res[b * slab_y:(b + 1) * slab_y, x * depth:(x + 1) * depth],
                    )

        loop(total_y // y_chunk, one)

    def pad_line(field, line, length):
        field[line, 0:PAD, :] = jnp.broadcast_to(field[line, PAD:PAD + 1, :], (PAD, depth))
        field[line, PAD + length:, :] = jnp.broadcast_to(
            field[line, PAD + length - 1:PAD + length, :], (PAD, depth)
        )

    def pad_field(field):
        for x in range(part_x):
            pad_line(field, x, total_y)

    def received_to_field(j, field):
        def one(c):
            for x in range(part_x):
                field[x, pl.ds(pl.multiple_of(PAD + c * slab_y, 8), slab_y), :] = cr[
                    j, c * part_x + x
                ].astype(F32)

        loop(cols, one, 2)
        pad_field(field)

    def three(field, x, c):
        base = pl.multiple_of(PAD + c * slab_y, 8)
        return (
            field[x, pl.ds(base - 1, slab_y), :],
            field[x, pl.ds(base, slab_y), :],
            field[x, pl.ds(base + 1, slab_y), :],
        )

    def apply_lines(field, faces, x, c):
        below, mid, above = three(field, x, c)
        face_below, face, _ = three(faces, x, c)
        return mid + face * (above - mid) - face_below * (mid - below)

    def apply_y(field, x, c):
        return apply_lines(field, cfy, x, c)

    def cells_line(field, grad, x, c):
        below, mid, above = three(field, x, c)
        g_below, g_mid, g_above = three(grad, x, c)
        return (above - mid) * (g_above - g_mid) + (mid - below) * (g_mid - g_below)

    def faces_line(field, faces, x, c):
        _, mid, above = three(field, x, c)
        faces[x, rows_of(c), :] = HALF_STEP * (mid + above)

    def close_faces(faces, x, length):
        faces[x, 0:PAD, :] = jnp.zeros((PAD, depth), F32)
        faces[x, PAD + length - 1:PAD + length, :] = jnp.zeros((1, depth), F32)
        faces[x, PAD + length:, :] = jnp.zeros((PAD, depth), F32)

    def cells_z(state, backed):
        first = next_lane(state) - state
        second = next_lane(backed) - backed
        return 2.0 * first * second * lane_mask(state.shape)

    def set_src_y(x, c, values):
        src_y[pl.ds(pl.multiple_of(c * slab_y, slab_y), slab_y), x * depth:(x + 1) * depth] = (
            values.astype(BF)
        )

    def source_y(field):
        def one(c):
            for x in range(part_x):
                set_src_y(x, c, apply_y(field, x, c))

        loop(cols, one)

    def low_codes(zones):
        code = jnp.broadcast_to(zones & (depth - 1), (depth, depth))
        return jnp.where(
            code == lax.broadcasted_iota(jnp.int32, (depth, depth), 0), 1.0, 0.0
        ).astype(BF)

    def high_codes(zones):
        code = jnp.broadcast_to(zones // depth, (16, depth))
        return jnp.where(code == lax.broadcasted_iota(jnp.int32, (16, depth), 0), 1.0, 0.0)

    def spread(sums, zones):
        both = jnp.concatenate([sums, sums], axis=0) * high_codes(zones)
        high, low = split_two(both)
        return jnp.concatenate([high, low], axis=0)

    def lanes(index):
        return pl.ds(pl.multiple_of(index * depth, depth), depth)

    def set_codes():
        groups = 8 // part_x
        for x in range(part_x):
            line = jnp.zeros((1, total_y), jnp.int32)
            for g in range(groups):
                mine = jnp.where(lax.rem(col, groups) == g, 1, 0)
                line = line + mine * zone_y[g * part_x + x:g * part_x + x + 1, :]
            for c in range(cols):
                index = c * part_x + x
                zone_lines[index:index + 1, :] = line[:, c * slab_y:(c + 1) * slab_y]
        for c in range(chunks_x):
            block = zone_block[c * chunk:(c + 1) * chunk, :].astype(F32)
            zone_turned[c] = jnp.transpose(block)
        for h in range(2):
            for y in range(piece_y):
                for c in range(chunks_x):
                    index = (h * piece_y + y) * chunks_x + c
                    place = pl.ds(h * half_y + row * piece_y + y, 1)
                    zone_cols[index:index + 1, :] = zone_turned[c, place, :].astype(jnp.int32)

        def one(i):
            lo_x[:, lanes(i)] = low_codes(zone_cols[pl.ds(i, 1), :])
            lo_y[:, lanes(i)] = low_codes(zone_lines[pl.ds(i, 1), :])
            own = owner[pl.ds(i, 1), :]
            lo_own[:, lanes(i)] = low_codes(own)
            hi_own[:, lanes(i)] = high_codes(own)

        loop(16, one)

    def zones_x(field, grad, h):
        def one(c):
            for y in range(piece_y):
                line = h * piece_y + y
                index = line * chunks_x + c
                spread_x[:, lanes(index)] = spread(
                    depth_sum(cells_line(field, grad, line, c)), zone_cols[pl.ds(index, 1), :]
                )

        loop(chunks_x, one, 2)
        count = piece_y * chunks_x * depth
        part = slice(h * count, (h + 1) * count)
        zacc[...] += dot_nt(spread_x[:, part], lo_x[:, part])

    def zones_y(field, grad, state, back):
        def one(c):
            for x in range(part_x):
                index = c * part_x + x
                cells = cells_line(field, grad, x, c)
                cells = cells + cells_z(state[index].astype(F32), back[index])
                spread_y[:, lanes(index)] = spread(
                    depth_sum(cells), zone_lines[pl.ds(index, 1), :]
                )

        loop(cols, one)
        zacc[...] += dot_nt(spread_y[...], lo_y[...])

    def back_z(j, back):
        def one(c):
            for x in range(part_x):
                index = c * part_x + x
                backed = dot_nn(cr[j, index], lz[...])
                back[index] = backed
                set_src_y(x, c, apply_z(backed, cfz_y[index]))

        loop(cols, one, 2)

    def back_y(j, grad):
        line_y_to_field(grad)

        def one(c):
            for x in range(part_x):
                cs[j, c * part_x + x] = apply_y(grad, x, c).astype(BF)

        loop(cols, one)
        send_col(j, 0, cs.at[j], all_y)
        keep_own(j, cs.at[j], all_y)

    loads[0].wait()
    half_planes_to_send(cond, 0, 0)
    pl.semaphore_wait(barrier, rows + cols - 2)
    send_row(0, 0)
    loads[1].wait()
    half_planes_to_send(head, 1, 0)
    send_row(1, 0)
    send_col(0, 0, cond_hbm, all_y)
    send_col(1, 0, cot_hbm, all_y)
    half_planes_to_send(cond, 0, 1)
    send_row(0, 1)
    half_planes_to_send(head, 1, 1)
    send_row(1, 1)

    for slot in (2, 3, 4, 5, 6):
        loads[slot].wait()
    col_wait(0, 0, all_y).wait_recv()
    received_to_field(0, field1)

    def faces_y(c):
        for x in range(part_x):
            index = c * part_x + x
            own = cr[0, index].astype(F32)
            cfz_y[index] = HALF_STEP * (own + next_lane(own)) * lane_mask(own.shape)
            faces_line(field1, cfy, x, c)

    loop(cols, faces_y)
    for x in range(part_x):
        close_faces(cfy, x, total_y)
    col_wait(1, 0, all_y).wait_recv()
    back_z(1, back5)
    back_y(2, grad4)

    zacc[...] = jnp.zeros(zacc.shape, F32)
    for h in range(2):
        row_wait(0, h).wait_recv()
        received_to_field_x(0, h, field3)

        def faces_x(y, c):
            faces_line(field3, cfx, h * piece_y + y, c)

        each_x(faces_x)
        for y in range(piece_y):
            close_faces(cfx, h * piece_y + y, total_x)
        row_wait(1, h).wait_recv()
        forward_x(1, 2, h, field0)
    for slot in (7, 8, 9):
        loads[slot].wait()
    set_codes()

    col_wait(2, 0, all_y).wait_recv()
    hub_planes_to_send(cr.at[2], 3)
    for h in range(2):
        row_wait(2, h).wait_recv()
        send_row(3, h)
        hub_to_lines(2, 3, h)

    row_wait(3, 0).wait_recv()
    adjoint_x(3, 4, 0, grad3)

    for h in range(2):
        col_wait(3, h, half(h)).wait_recv()
    received_to_field(3, field1)
    source_y(field1)

    def state3_block(index, state):
        state2[index] = state
        source = apply_z(state.astype(F32), cfz_y[index]).astype(BF)
        cs[4, index] = dot_nt(source, lz[...]).astype(BF)

    line_y_to_blocks(state3_block)
    send_col(4, 0, cs.at[4], all_y)
    keep_own(4, cs.at[4], all_y)

    row_wait(3, 1).wait_recv()
    adjoint_x(3, 4, 1, grad3)
    col_wait(4, 0, all_y).wait_recv()
    hub_planes_to_send(cr.at[4], 5)

    for h in range(2):
        row_wait(4, h).wait_recv()
        send_row(5, h)
        hub_to_lines(4, 5, h)

    row_wait(5, 0).wait_recv()
    forward_x(5, 6, 0, field3)

    for h in range(2):
        col_wait(5, h, half(h)).wait_recv()
    back_z(5, back2)
    back_y(6, grad1)

    row_wait(5, 1).wait_recv()
    forward_x(5, 6, 1, field3)
    zones_x(field3, grad3, 0)
    zones_x(field3, grad3, 1)
    col_wait(6, 0, all_y).wait_recv()
    hub_planes_to_send(cr.at[6], 7)

    for h in range(2):
        row_wait(6, h).wait_recv()
        send_row(7, h)
        hub_to_lines(6, 7, h)
    zones_y(field1, grad1, state2, back2)

    row_wait(7, 0).wait_recv()
    adjoint_x(7, 8, 0, grad0)
    zones_x(field0, grad0, 0)

    for h in range(2):
        col_wait(7, h, half(h)).wait_recv()
    received_to_field(7, field4)
    source_y(field4)

    def state5_block(index, state):
        state5[index] = state

    line_y_to_blocks(state5_block)
    zones_y(field4, grad4, state5, back5)

    row_wait(7, 1).wait_recv()
    back_x(7, 1, grad0)
    zones_x(field0, grad0, 1)

    sums = (zacc[0:16, :] + zacc[16:32, :]) * (-HALF_STEP * scale)
    high, low = split_two(sums)
    ordered = dot_nn(jnp.concatenate([high, low], axis=0), lo_own[...])
    ordered = (ordered[0:16] + ordered[16:32]) * hi_own[...]
    ordered = jnp.sum(ordered, axis=0, keepdims=True)
    for g in range(z_send.shape[0]):
        z_send[g] = ordered[:, g * depth:(g + 1) * depth]

    def send_zone_row(i):
        r = row_peer(i + 1)
        pltpu.make_async_remote_copy(
            src_ref=z_send.at[r // 2], dst_ref=z_row.at[row],
            send_sem=zs_sem.at[0], recv_sem=zr_sem.at[0],
            device_id=(r, col), device_id_type=MESH,
        ).start()

    loop(rows - 1, send_zone_row)
    z_row[row] = z_send[row // 2]
    flux_x(8, 1, grad0)

    def zone_wait(phase, ref, count):
        part = pl.ds(0, count)
        return pltpu.make_async_remote_copy(
            src_ref=ref.at[part], dst_ref=ref.at[part],
            send_sem=zs_sem.at[phase], recv_sem=zr_sem.at[phase],
            device_id=(row, col), device_id_type=MESH,
        )

    zone_wait(0, z_row, rows - 1).wait_recv()
    z_mid[...] = jnp.sum(z_row[...], axis=0)

    def send_zone_col(i):
        c = col_peer(i + 1)
        pltpu.make_async_remote_copy(
            src_ref=z_mid, dst_ref=z_col.at[col],
            send_sem=zs_sem.at[1], recv_sem=zr_sem.at[1],
            device_id=(row, c), device_id_type=MESH,
        ).start()

    loop(cols - 1, send_zone_col)
    z_col[col] = z_mid[...]
    row_wait(8, 0).wait_recv()
    out_ref[0] = rr[8, 0]
    zone_wait(1, z_col, cols - 1).wait_recv()
    final = jnp.sum(z_col[...], axis=0)
    offset = lax.rem(row, 2) * (depth // 2) + col * 8
    final = jnp.broadcast_to(final, zout_ref.shape)
    zout_ref[...] = pltpu.roll(final, lax.rem(depth - offset, depth), axis=1)
    row_wait(8, 1).wait_recv()
    out_ref[1] = rr[8, 1]

    for k in range(9):
        for h in range(2):
            row_wait(k, h).wait_send()
    for j in (0, 1, 2, 4, 6):
        col_wait(j, 0, all_y).wait_send()
    for j in (3, 5, 7):
        for h in range(2):
            col_wait(j, h, half(h)).wait_send()
    zone_wait(0, z_row, rows - 1).wait_send()
    zone_wait(1, z_col, cols - 1).wait_send()


def finish(turned_ref, zones_ref, out_ref, zout_ref, turn):
    slab_x, slab_y, depth = out_ref.shape
    count = slab_x * slab_y
    turn[...] = turned_ref[...].reshape(count, depth).astype(F32)

    def one(x):
        out_ref[x] = turn[pl.ds(x, slab_y, stride=slab_x), :].astype(BF)

    loop(slab_x, one, 4)
    zout_ref[...] = zones_ref[0, 0:zout_ref.shape[0]]


def on_device(
    rows, cols, head_start, cotangent, conductivity, line_x, line_y, line_z, zone_map, owner_order
):
    slab_x, slab_y, depth = head_start.shape
    total_x, total_y = zone_map.shape
    zone_count = owner_order.shape[0]
    part_x = slab_x // cols
    part_y = slab_y // rows
    scale = 1.0 / math.sqrt(total_x * total_y * depth / zone_count)
    groups = zone_count // depth
    lines_x = pltpu.VMEM((part_y, total_x + 2 * PAD, depth), F32)
    lines_y = pltpu.VMEM((part_x, total_y + 2 * PAD, depth), F32)
    slab16 = pltpu.VMEM((slab_x, slab_y, depth), BF)
    slab32 = pltpu.VMEM((slab_x, slab_y, depth), F32)
    codes = pltpu.VMEM((depth, slab_x * slab_y), BF)
    spread = pltpu.VMEM((32, slab_x * slab_y), BF)
    row_slots = pltpu.VMEM((9, 2, rows, part_y // 2, slab_x, depth), BF)
    col_slots = pltpu.VMEM((8, slab_x, slab_y, depth), BF)
    scratch = [
        slab16, slab16,
        pltpu.VMEM(line_x.shape, BF),
        pltpu.VMEM(line_y.shape, BF),
        pltpu.VMEM(line_z.shape, BF),
        pltpu.VMEM((total_x, slab_y), jnp.int32),
        pltpu.VMEM((total_x // 128, slab_y, 128), F32),
        pltpu.VMEM((8, total_y), jnp.int32),
        pltpu.VMEM((groups, depth), jnp.int32),
        row_slots, row_slots, col_slots, col_slots,
        pltpu.VMEM((slab_x * slab_y, depth), F32),
        lines_x, lines_y, slab32,
        lines_x, lines_x, lines_x, lines_x,
        lines_y, lines_y, lines_y, lines_y,
        slab32, slab32, slab16, slab16,
        pltpu.VMEM((total_x, part_y // 2 * depth), BF),
        pltpu.VMEM((total_y, part_x * depth), BF),
        pltpu.VMEM((16, depth), jnp.int32),
        pltpu.VMEM((16, depth), jnp.int32),
        codes, codes, codes,
        pltpu.VMEM((16, zone_count), F32),
        spread, spread,
        pltpu.VMEM((32, depth), F32),
        pltpu.VMEM((groups, 1, depth), F32),
        pltpu.VMEM((1, depth), F32),
        pltpu.VMEM((rows, 1, depth), F32),
        pltpu.VMEM((cols, 1, depth), F32),
        pltpu.SemaphoreType.DMA((10,)),
        pltpu.SemaphoreType.DMA((9, 2)),
        pltpu.SemaphoreType.DMA((9, 2)),
        pltpu.SemaphoreType.DMA((8, 2)),
        pltpu.SemaphoreType.DMA((8, 2)),
        pltpu.SemaphoreType.DMA((2,)),
        pltpu.SemaphoreType.DMA((2,)),
    ]
    turned, zones = pl.pallas_call(
        functools.partial(kernel, rows, cols, scale),
        out_shape=(
            jax.ShapeDtypeStruct((2, rows, part_y // 2, slab_x, depth), BF),
            jax.ShapeDtypeStruct((8, depth), F32),
        ),
        in_specs=[pl.BlockSpec(memory_space=pl.ANY)] * 8,
        out_specs=(
            pl.BlockSpec(memory_space=pltpu.VMEM),
            pl.BlockSpec(memory_space=pltpu.VMEM),
        ),
        scratch_shapes=scratch,
        compiler_params=pltpu.CompilerParams(
            collective_id=0, has_side_effects=True, vmem_limit_bytes=56 << 20
        ),
        name="adjoint_lines",
    )(
        head_start, cotangent, conductivity, line_x, line_y, line_z, zone_map,
        owner_order.reshape(groups, depth),
    )
    vmem = pl.BlockSpec(memory_space=pltpu.VMEM)
    return pl.pallas_call(
        finish,
        out_shape=(
            jax.ShapeDtypeStruct((slab_x, slab_y, depth), BF),
            jax.ShapeDtypeStruct((zone_count // (rows * cols),), F32),
        ),
        in_specs=[vmem, vmem],
        out_specs=(vmem, vmem),
        scratch_shapes=[pltpu.VMEM((slab_x * slab_y, depth), F32)],
        name="finish_slab",
    )(turned, zones)


def solution(mesh):
    slab = P("row", "col", None)
    return jax.shard_map(
        functools.partial(on_device, mesh.shape["row"], mesh.shape["col"]),
        mesh=mesh,
        in_specs=(slab, slab, slab, P(), P(), P(), P(), P()),
        out_specs=(slab, P(("row", "col"))),
        check_vma=False,
    )
```

```python
import functools
import math

import jax
import jax.numpy as jnp
from jax import lax
from jax.experimental import pallas as pl
from jax.experimental.pallas import tpu as pltpu
from jax.sharding import PartitionSpec as P

MESH = pl.DeviceIdType.MESH
BF = jnp.bfloat16
F32 = jnp.float32
HALF_STEP = 0.075
PAD = 8


def dot_nn(a, b):
    return lax.dot_general(a, b, (((1,), (0,)), ((), ())), preferred_element_type=F32)


def dot_nt(a, b):
    return lax.dot_general(a, b, (((1,), (1,)), ((), ())), preferred_element_type=F32)


def dot_tn(a, b):
    return lax.dot_general(a, b, (((0,), (0,)), ((), ())), preferred_element_type=F32)


def loop(count, body, unroll=1):
    def step(i, carry):
        body(i)
        return carry

    lax.fori_loop(0, count, step, 0, unroll=unroll)


def split_two(values):
    high = values.astype(BF)
    low = (values - high.astype(F32)).astype(BF)
    return high, low


def kernel(
    rows, cols, scale,
    head_hbm, cot_hbm, cond_hbm, lx_hbm, ly_hbm, lz_hbm, zmap_hbm, owner_hbm,
    out_ref, zout_ref,
    head, cond, lx, ly, lz, zone_block, zone_turned, zone_y, owner,
    rs, rr, cs, cr, turn, cfx, cfy, cfz_y,
    field0, field3, grad3, grad0, field1, field4, grad4, grad1,
    back5, back2, state2, state5, src_x, src_y,
    zone_cols, zone_lines, lo_x, lo_y, lo_own, hi_own, spread_x, spread_y,
    zacc, z_send, z_mid, z_row, z_col,
    local_sem, rs_sem, rr_sem, cs_sem, cr_sem, zs_sem, zr_sem,
):
    row = lax.axis_index("row")
    col = lax.axis_index("col")
    slab_x, slab_y, depth = head_hbm.shape
    part_x = slab_x // cols
    total_x = lx.shape[0]
    total_y = ly.shape[0]
    half_y = slab_y // 2
    piece_y = half_y // rows

    def row_peer(i):
        return lax.rem(row + i, rows)

    def col_peer(i):
        return lax.rem(col + i, cols)

    barrier = pltpu.get_barrier_semaphore()

    def greet_row(i):
        pl.semaphore_signal(barrier, inc=1, device_id=(row_peer(i + 1), col), device_id_type=MESH)

    def greet_col(i):
        pl.semaphore_signal(barrier, inc=1, device_id=(row, col_peer(i + 1)), device_id_type=MESH)

    loop(rows - 1, greet_row, rows - 1)
    loop(cols - 1, greet_col, cols - 1)

    loads = {}

    def load(slot, src, dst):
        copy = pltpu.make_async_copy(src, dst, local_sem.at[slot])
        copy.start()
        loads[slot] = copy

    own_x = pl.ds(col * part_x, part_x)
    load(0, cond_hbm, cond)
    load(1, head_hbm, head)

    def near_last(k, count):
        return count // 2 + ((k + 1) // 2) * (1 - 2 * lax.rem(k, 2))

    ring_x = 4
    side = lax.rem(col, 2)
    ring_z = rows // ring_x

    def send_row(k, h):
        def one(shift_z, shift_x):
            z = lax.rem(row // ring_x + shift_z + side * (ring_z - 2 * shift_z), ring_z)
            x = lax.rem(lax.rem(row, ring_x) + shift_x + side * (ring_x - 2 * shift_x), ring_x)
            r = z * ring_x + x
            pltpu.make_async_remote_copy(
                src_ref=rs.at[k, h, r], dst_ref=rr.at[k, h, row],
                send_sem=rs_sem.at[k, h], recv_sem=rr_sem.at[k, h],
                device_id=(r, col), device_id_type=MESH,
            ).start()

        shifts_z = [ring_z // 2 + ((i + 1) // 2) * (1 - 2 * (i % 2)) for i in range(ring_z)]

        def lines(i):
            for shift_z in shifts_z:
                one(shift_z, near_last(i, ring_x))

        loop(ring_x - 1, lines)
        for shift_z in shifts_z[:-1]:
            one(shift_z, 0)
        rr[k, h, row] = rs[k, h, row]

    def row_wait(k, h):
        part = pl.ds(0, rows - 1)
        return pltpu.make_async_remote_copy(
            src_ref=rs.at[k, h, part], dst_ref=rr.at[k, h, part],
            send_sem=rs_sem.at[k, h], recv_sem=rr_sem.at[k, h],
            device_id=(row, col), device_id_type=MESH,
        )

    all_y = pl.ds(0, slab_y)

    def half(h):
        return pl.ds(h * half_y, half_y)

    def send_col(j, slot, src, ys):
        def one(i):
            c = col_peer(i + 1)
            pltpu.make_async_remote_copy(
                src_ref=src.at[pl.ds(c * part_x, part_x), ys],
                dst_ref=cr.at[j, own_x, ys],
                send_sem=cs_sem.at[j, slot], recv_sem=cr_sem.at[j, slot],
                device_id=(row, c), device_id_type=MESH,
            ).start()

        loop(cols - 1, one)

    def keep_own(j, src, ys):
        cr[j, own_x, ys] = src[own_x, ys]

    def col_wait(j, slot, ys):
        part = pl.ds(0, (cols - 1) * part_x)
        return pltpu.make_async_remote_copy(
            src_ref=cr.at[j, part, ys], dst_ref=cr.at[j, part, ys],
            send_sem=cs_sem.at[j, slot], recv_sem=cr_sem.at[j, slot],
            device_id=(row, col), device_id_type=MESH,
        )

    def next_lane(f):
        return pltpu.roll(f, f.shape[1] - 1, axis=1)

    def prev_lane(f):
        return pltpu.roll(f, 1, axis=1)

    def apply_z(f, faces):
        flux = faces * (next_lane(f) - f)
        return f + flux - prev_lane(flux)

    def lane_mask(shape):
        lane = lax.broadcasted_iota(jnp.int32, shape, 1)
        return jnp.where(lane < depth - 1, 1.0, 0.0).astype(F32)

    ones8 = jnp.ones((8, 2 * depth), BF)

    def depth_sum(products):
        high, low = split_two(products)
        return dot_nt(ones8, jnp.concatenate([high, low], axis=1))

    def turn_in(x, h, plane):
        turn[pl.ds(h * half_y * slab_x + x, half_y, stride=slab_x), :] = plane

    def turn_out(x, h):
        return turn[pl.ds(h * half_y * slab_x + x, half_y, stride=slab_x), :]

    group = 4
    block = group * piece_y * slab_x

    def turned_to_send(k, h):
        def one(g):
            base = pl.multiple_of(h * half_y * slab_x + g * block, block)
            piece = turn[pl.ds(base, block), :].astype(BF)
            rs[k, h, pl.ds(g * group, group)] = piece.reshape(group, piece_y, slab_x, depth)

        loop(rows // group, one, 2)

    def received_to_turn(k, h):
        def one(g):
            base = pl.multiple_of(h * half_y * slab_x + g * block, block)
            piece = rr[k, h, pl.ds(g * group, group)].reshape(block, depth)
            turn[pl.ds(base, block), :] = piece.astype(F32)

        loop(rows // group, one, 2)

    def received_to_planes(k, h, buf, offset):
        received_to_turn(k, h)

        def one(x):
            buf[offset + x, half(h)] = turn_out(x, h).astype(BF)

        loop(slab_x, one, 4)

    def half_planes_to_send(buf, k, h):
        def one(x):
            turn_in(x, h, buf[x, half(h)].astype(F32))

        loop(slab_x, one, 4)
        turned_to_send(k, h)

    def hub_planes_to_send(buf, k):
        for h in range(2):
            half_planes_to_send(buf, k, h)

    def hub_to_lines(k, j, h):
        buf = cs.at[j]
        received_to_planes(k, h, buf, 0)
        send_col(j, h, buf, half(h))
        keep_own(j, buf, half(h))

    chunk = 128
    peers_chunk = chunk // slab_x
    chunks_x = total_x // chunk

    def received_x(k, h, y, c):
        return rr[k, h, pl.ds(c * peers_chunk, peers_chunk), y].reshape(chunk, depth)

    def to_send_x(k, h, y, c, values):
        rs[k, h, pl.ds(c * peers_chunk, peers_chunk), y] = values.astype(BF).reshape(
            peers_chunk, slab_x, depth
        )

    def rows_of(c):
        return pl.ds(pl.multiple_of(PAD + c * chunk, 8), chunk)

    def each_x(body, unroll=1):
        def one(c):
            for y in range(piece_y):
                body(y, c)

        loop(chunks_x, one, unroll)

    def pad_lines_x(field, h):
        for y in range(piece_y):
            pad_line(field, h * piece_y + y, total_x)

    def received_to_field_x(k, h, field):
        def one(y, c):
            field[h * piece_y + y, rows_of(c), :] = received_x(k, h, y, c).astype(F32)

        each_x(one)
        pad_lines_x(field, h)

    def src_part(c):
        return pl.ds(pl.multiple_of(c * chunk, chunk), chunk)

    def forward_x(k_in, k_out, h, field):
        received_to_field_x(k_in, h, field)

        def source(y, c):
            src_x[src_part(c), y * depth:(y + 1) * depth] = apply_lines(
                field, cfx, h * piece_y + y, c
            ).astype(BF)

        each_x(source)

        def line(c):
            res = dot_nn(lx[src_part(c), :], src_x[...])
            for y in range(piece_y):
                to_send_x(k_out, h, y, c, res[:, y * depth:(y + 1) * depth])

        loop(chunks_x, line, 2)
        send_row(k_out, h)

    def back_x(k_in, h, grad):
        rhs = jnp.concatenate(
            [rr[k_in, h, :, y].reshape(total_x, depth) for y in range(piece_y)], axis=1
        )

        def line(c):
            res = dot_tn(lx[:, src_part(c)], rhs)
            for y in range(piece_y):
                grad[h * piece_y + y, rows_of(c), :] = res[:, y * depth:(y + 1) * depth]

        loop(chunks_x, line, 2)
        pad_lines_x(grad, h)

    def flux_x(k_out, h, grad):
        def flux(y, c):
            to_send_x(k_out, h, y, c, apply_lines(grad, cfx, h * piece_y + y, c))

        each_x(flux)
        send_row(k_out, h)

    def adjoint_x(k_in, k_out, h, grad):
        back_x(k_in, h, grad)
        flux_x(k_out, h, grad)

    y_chunk = 256
    blocks = y_chunk // slab_y

    def line_y_chunk(m, transpose):
        part = pl.ds(pl.multiple_of(m * y_chunk, y_chunk), y_chunk)
        if transpose:
            return dot_tn(ly[:, part], src_y[...])
        return dot_nn(ly[part, :], src_y[...])

    def line_y_to_field(field):
        def one(m):
            res = line_y_chunk(m, True)
            for x in range(part_x):
                field[x, pl.ds(pl.multiple_of(PAD + m * y_chunk, 8), y_chunk), :] = res[
                    :, x * depth:(x + 1) * depth
                ]

        loop(total_y // y_chunk, one)
        pad_field(field)

    def line_y_to_blocks(body):
        def one(m):
            res = line_y_chunk(m, False).astype(BF)
            for b in range(blocks):
                for x in range(part_x):
                    body(
                        (m * blocks + b) * part_x + x,
                        res[b * slab_y:(b + 1) * slab_y, x * depth:(x + 1) * depth],
                    )

        loop(total_y // y_chunk, one)

    def pad_line(field, line, length):
        field[line, 0:PAD, :] = jnp.broadcast_to(field[line, PAD:PAD + 1, :], (PAD, depth))
        field[line, PAD + length:, :] = jnp.broadcast_to(
            field[line, PAD + length - 1:PAD + length, :], (PAD, depth)
        )

    def pad_field(field):
        for x in range(part_x):
            pad_line(field, x, total_y)

    def received_to_field(j, field):
        def one(c):
            for x in range(part_x):
                field[x, pl.ds(pl.multiple_of(PAD + c * slab_y, 8), slab_y), :] = cr[
                    j, c * part_x + x
                ].astype(F32)

        loop(cols, one, 2)
        pad_field(field)

    def three(field, x, c):
        base = pl.multiple_of(PAD + c * slab_y, 8)
        return (
            field[x, pl.ds(base - 1, slab_y), :],
            field[x, pl.ds(base, slab_y), :],
            field[x, pl.ds(base + 1, slab_y), :],
        )

    def apply_lines(field, faces, x, c):
        below, mid, above = three(field, x, c)
        face_below, face, _ = three(faces, x, c)
        return mid + face * (above - mid) - face_below * (mid - below)

    def apply_y(field, x, c):
        return apply_lines(field, cfy, x, c)

    def cells_line(field, grad, x, c):
        below, mid, above = three(field, x, c)
        g_below, g_mid, g_above = three(grad, x, c)
        return (above - mid) * (g_above - g_mid) + (mid - below) * (g_mid - g_below)

    def faces_line(field, faces, x, c):
        _, mid, above = three(field, x, c)
        faces[x, rows_of(c), :] = HALF_STEP * (mid + above)

    def close_faces(faces, x, length):
        faces[x, 0:PAD, :] = jnp.zeros((PAD, depth), F32)
        faces[x, PAD + length - 1:PAD + length, :] = jnp.zeros((1, depth), F32)
        faces[x, PAD + length:, :] = jnp.zeros((PAD, depth), F32)

    def cells_z(state, backed):
        first = next_lane(state) - state
        second = next_lane(backed) - backed
        return 2.0 * first * second * lane_mask(state.shape)

    def set_src_y(x, c, values):
        src_y[pl.ds(pl.multiple_of(c * slab_y, slab_y), slab_y), x * depth:(x + 1) * depth] = (
            values.astype(BF)
        )

    def source_y(field):
        def one(c):
            for x in range(part_x):
                set_src_y(x, c, apply_y(field, x, c))

        loop(cols, one)

    def low_codes(zones):
        code = jnp.broadcast_to(zones & (depth - 1), (depth, depth))
        return jnp.where(
            code == lax.broadcasted_iota(jnp.int32, (depth, depth), 0), 1.0, 0.0
        ).astype(BF)

    def high_codes(zones):
        code = jnp.broadcast_to(zones // depth, (16, depth))
        return jnp.where(code == lax.broadcasted_iota(jnp.int32, (16, depth), 0), 1.0, 0.0)

    def spread(sums, zones):
        both = jnp.concatenate([sums, sums], axis=0) * high_codes(zones)
        high, low = split_two(both)
        return jnp.concatenate([high, low], axis=0)

    def lanes(index):
        return pl.ds(pl.multiple_of(index * depth, depth), depth)

    def set_codes():
        groups = 8 // part_x
        for x in range(part_x):
            line = jnp.zeros((1, total_y), jnp.int32)
            for g in range(groups):
                mine = jnp.where(lax.rem(col, groups) == g, 1, 0)
                line = line + mine * zone_y[g * part_x + x:g * part_x + x + 1, :]
            for c in range(cols):
                index = c * part_x + x
                zone_lines[index:index + 1, :] = line[:, c * slab_y:(c + 1) * slab_y]
        for c in range(chunks_x):
            block = zone_block[c * chunk:(c + 1) * chunk, :].astype(F32)
            zone_turned[c] = jnp.transpose(block)
        for h in range(2):
            for y in range(piece_y):
                for c in range(chunks_x):
                    index = (h * piece_y + y) * chunks_x + c
                    place = pl.ds(h * half_y + row * piece_y + y, 1)
                    zone_cols[index:index + 1, :] = zone_turned[c, place, :].astype(jnp.int32)

        def one(i):
            lo_x[:, lanes(i)] = low_codes(zone_cols[pl.ds(i, 1), :])
            lo_y[:, lanes(i)] = low_codes(zone_lines[pl.ds(i, 1), :])
            own = owner[pl.ds(i, 1), :]
            lo_own[:, lanes(i)] = low_codes(own)
            hi_own[:, lanes(i)] = high_codes(own)

        loop(16, one)

    def zones_x(field, grad, h):
        def one(c):
            for y in range(piece_y):
                line = h * piece_y + y
                index = line * chunks_x + c
                spread_x[:, lanes(index)] = spread(
                    depth_sum(cells_line(field, grad, line, c)), zone_cols[pl.ds(index, 1), :]
                )

        loop(chunks_x, one, 2)
        count = piece_y * chunks_x * depth
        part = slice(h * count, (h + 1) * count)
        zacc[...] += dot_nt(spread_x[:, part], lo_x[:, part])

    def zones_y(field, grad, state, back):
        def one(c):
            for x in range(part_x):
                index = c * part_x + x
                cells = cells_line(field, grad, x, c)
                cells = cells + cells_z(state[index].astype(F32), back[index])
                spread_y[:, lanes(index)] = spread(
                    depth_sum(cells), zone_lines[pl.ds(index, 1), :]
                )

        loop(cols, one)
        zacc[...] += dot_nt(spread_y[...], lo_y[...])

    def back_z(j, back):
        def one(c):
            for x in range(part_x):
                index = c * part_x + x
                backed = dot_nn(cr[j, index], lz[...])
                back[index] = backed
                set_src_y(x, c, apply_z(backed, cfz_y[index]))

        loop(cols, one, 2)

    def back_y(j, grad):
        line_y_to_field(grad)

        def one(c):
            for x in range(part_x):
                cs[j, c * part_x + x] = apply_y(grad, x, c).astype(BF)

        loop(cols, one)
        send_col(j, 0, cs.at[j], all_y)
        keep_own(j, cs.at[j], all_y)

    loads[0].wait()
    half_planes_to_send(cond, 0, 0)
    pl.semaphore_wait(barrier, rows + cols - 2)
    send_row(0, 0)
    loads[1].wait()
    half_planes_to_send(head, 1, 0)
    send_row(1, 0)
    load(2, cond_hbm.at[own_x], cr.at[0, own_x])
    load(3, cot_hbm.at[own_x], cr.at[1, own_x])
    load(4, lz_hbm, lz)
    load(5, lx_hbm, lx)
    load(6, ly_hbm, ly)
    load(7, zmap_hbm.at[:, pl.ds(pl.multiple_of(col * slab_y, slab_y), slab_y)], zone_block)
    load(8, zmap_hbm.at[pl.ds(row * slab_x + (col * part_x // 8) * 8, 8)], zone_y)
    load(9, owner_hbm, owner)
    send_col(0, 0, cond_hbm, all_y)
    send_col(1, 0, cot_hbm, all_y)
    half_planes_to_send(cond, 0, 1)
    send_row(0, 1)
    half_planes_to_send(head, 1, 1)
    send_row(1, 1)

    for slot in (2, 3, 4, 5, 6):
        loads[slot].wait()
    col_wait(0, 0, all_y).wait_recv()
    received_to_field(0, field1)

    def faces_y(c):
        for x in range(part_x):
            index = c * part_x + x
            own = cr[0, index].astype(F32)
            cfz_y[index] = HALF_STEP * (own + next_lane(own)) * lane_mask(own.shape)
            faces_line(field1, cfy, x, c)

    loop(cols, faces_y)
    for x in range(part_x):
        close_faces(cfy, x, total_y)
    col_wait(1, 0, all_y).wait_recv()
    back_z(1, back5)
    back_y(2, grad4)

    zacc[...] = jnp.zeros(zacc.shape, F32)
    for h in range(2):
        row_wait(0, h).wait_recv()
        received_to_field_x(0, h, field3)

        def faces_x(y, c):
            faces_line(field3, cfx, h * piece_y + y, c)

        each_x(faces_x)
        for y in range(piece_y):
            close_faces(cfx, h * piece_y + y, total_x)
        row_wait(1, h).wait_recv()
        forward_x(1, 2, h, field0)
    for slot in (7, 8, 9):
        loads[slot].wait()
    set_codes()

    col_wait(2, 0, all_y).wait_recv()
    hub_planes_to_send(cr.at[2], 3)
    for h in range(2):
        row_wait(2, h).wait_recv()
        send_row(3, h)
        hub_to_lines(2, 3, h)

    row_wait(3, 0).wait_recv()
    adjoint_x(3, 4, 0, grad3)

    for h in range(2):
        col_wait(3, h, half(h)).wait_recv()
    received_to_field(3, field1)
    source_y(field1)

    def state3_block(index, state):
        state2[index] = state
        source = apply_z(state.astype(F32), cfz_y[index]).astype(BF)
        cs[4, index] = dot_nt(source, lz[...]).astype(BF)

    line_y_to_blocks(state3_block)
    send_col(4, 0, cs.at[4], all_y)
    keep_own(4, cs.at[4], all_y)

    row_wait(3, 1).wait_recv()
    adjoint_x(3, 4, 1, grad3)
    col_wait(4, 0, all_y).wait_recv()
    hub_planes_to_send(cr.at[4], 5)

    for h in range(2):
        row_wait(4, h).wait_recv()
        send_row(5, h)
        hub_to_lines(4, 5, h)

    row_wait(5, 0).wait_recv()
    forward_x(5, 6, 0, field3)

    for h in range(2):
        col_wait(5, h, half(h)).wait_recv()
    back_z(5, back2)
    back_y(6, grad1)

    row_wait(5, 1).wait_recv()
    forward_x(5, 6, 1, field3)
    zones_x(field3, grad3, 0)
    zones_x(field3, grad3, 1)
    col_wait(6, 0, all_y).wait_recv()
    hub_planes_to_send(cr.at[6], 7)

    for h in range(2):
        row_wait(6, h).wait_recv()
        send_row(7, h)
        hub_to_lines(6, 7, h)
    zones_y(field1, grad1, state2, back2)

    row_wait(7, 0).wait_recv()
    adjoint_x(7, 8, 0, grad0)
    zones_x(field0, grad0, 0)

    for h in range(2):
        col_wait(7, h, half(h)).wait_recv()
    received_to_field(7, field4)
    source_y(field4)

    def state5_block(index, state):
        state5[index] = state

    line_y_to_blocks(state5_block)
    zones_y(field4, grad4, state5, back5)

    row_wait(7, 1).wait_recv()
    back_x(7, 1, grad0)
    zones_x(field0, grad0, 1)

    def leave(h):
        received_to_planes(8, h, cs.at[0], 0)
        load(10 + h, cs.at[0, :, half(h)], out_ref.at[:, half(h)])

    sums = (zacc[0:16, :] + zacc[16:32, :]) * (-HALF_STEP * scale)
    high, low = split_two(sums)
    ordered = dot_nn(jnp.concatenate([high, low], axis=0), lo_own[...])
    ordered = (ordered[0:16] + ordered[16:32]) * hi_own[...]
    ordered = jnp.sum(ordered, axis=0, keepdims=True)
    for g in range(z_send.shape[0]):
        z_send[g] = ordered[:, g * depth:(g + 1) * depth]

    def send_zone_row(i):
        r = row_peer(i + 1)
        pltpu.make_async_remote_copy(
            src_ref=z_send.at[r // 2], dst_ref=z_row.at[row],
            send_sem=zs_sem.at[0], recv_sem=zr_sem.at[0],
            device_id=(r, col), device_id_type=MESH,
        ).start()

    loop(rows - 1, send_zone_row)
    z_row[row] = z_send[row // 2]
    flux_x(8, 1, grad0)

    def zone_wait(phase, ref, count):
        part = pl.ds(0, count)
        return pltpu.make_async_remote_copy(
            src_ref=ref.at[part], dst_ref=ref.at[part],
            send_sem=zs_sem.at[phase], recv_sem=zr_sem.at[phase],
            device_id=(row, col), device_id_type=MESH,
        )

    zone_wait(0, z_row, rows - 1).wait_recv()
    z_mid[...] = jnp.sum(z_row[...], axis=0)

    def send_zone_col(i):
        c = col_peer(i + 1)
        pltpu.make_async_remote_copy(
            src_ref=z_mid, dst_ref=z_col.at[col],
            send_sem=zs_sem.at[1], recv_sem=zr_sem.at[1],
            device_id=(row, c), device_id_type=MESH,
        ).start()

    loop(cols - 1, send_zone_col)
    z_col[col] = z_mid[...]
    row_wait(8, 0).wait_recv()
    leave(0)
    zone_wait(1, z_col, cols - 1).wait_recv()
    final = jnp.sum(z_col[...], axis=0)
    offset = lax.rem(row, 2) * (depth // 2) + col * 8
    final = jnp.broadcast_to(final, zout_ref.shape)
    zout_ref[...] = pltpu.roll(final, lax.rem(depth - offset, depth), axis=1)
    row_wait(8, 1).wait_recv()
    leave(1)
    for h in range(2):
        loads[10 + h].wait()

    for k in range(9):
        for h in range(2):
            row_wait(k, h).wait_send()
    for j in (0, 1, 2, 4, 6):
        col_wait(j, 0, all_y).wait_send()
    for j in (3, 5, 7):
        for h in range(2):
            col_wait(j, h, half(h)).wait_send()
    zone_wait(0, z_row, rows - 1).wait_send()
    zone_wait(1, z_col, cols - 1).wait_send()


def finish(slab_ref, zones_ref, out_ref, zout_ref):
    out_ref[...] = slab_ref[...]
    zout_ref[...] = zones_ref[0, 0:zout_ref.shape[0]]


def on_device(
    rows, cols, head_start, cotangent, conductivity, line_x, line_y, line_z, zone_map, owner_order
):
    slab_x, slab_y, depth = head_start.shape
    total_x, total_y = zone_map.shape
    zone_count = owner_order.shape[0]
    part_x = slab_x // cols
    part_y = slab_y // rows
    scale = 1.0 / math.sqrt(total_x * total_y * depth / zone_count)
    groups = zone_count // depth
    lines_x = pltpu.VMEM((part_y, total_x + 2 * PAD, depth), F32)
    lines_y = pltpu.VMEM((part_x, total_y + 2 * PAD, depth), F32)
    slab16 = pltpu.VMEM((slab_x, slab_y, depth), BF)
    slab32 = pltpu.VMEM((slab_x, slab_y, depth), F32)
    codes = pltpu.VMEM((depth, slab_x * slab_y), BF)
    spread = pltpu.VMEM((32, slab_x * slab_y), BF)
    row_slots = pltpu.VMEM((9, 2, rows, part_y // 2, slab_x, depth), BF)
    col_slots = pltpu.VMEM((8, slab_x, slab_y, depth), BF)
    scratch = [
        slab16, slab16,
        pltpu.VMEM(line_x.shape, BF),
        pltpu.VMEM(line_y.shape, BF),
        pltpu.VMEM(line_z.shape, BF),
        pltpu.VMEM((total_x, slab_y), jnp.int32),
        pltpu.VMEM((total_x // 128, slab_y, 128), F32),
        pltpu.VMEM((8, total_y), jnp.int32),
        pltpu.VMEM((groups, depth), jnp.int32),
        row_slots, row_slots, col_slots, col_slots,
        pltpu.VMEM((slab_x * slab_y + slab_x, depth), F32),
        lines_x, lines_y, slab32,
        lines_x, lines_x, lines_x, lines_x,
        lines_y, lines_y, lines_y, lines_y,
        slab32, slab32, slab16, slab16,
        pltpu.VMEM((total_x, part_y // 2 * depth), BF),
        pltpu.VMEM((total_y, part_x * depth), BF),
        pltpu.VMEM((16, depth), jnp.int32),
        pltpu.VMEM((16, depth), jnp.int32),
        codes, codes, codes,
        pltpu.VMEM((16, zone_count), F32),
        spread, spread,
        pltpu.VMEM((32, depth), F32),
        pltpu.VMEM((groups, 1, depth), F32),
        pltpu.VMEM((1, depth), F32),
        pltpu.VMEM((rows, 1, depth), F32),
        pltpu.VMEM((cols, 1, depth), F32),
        pltpu.SemaphoreType.DMA((12,)),
        pltpu.SemaphoreType.DMA((9, 2)),
        pltpu.SemaphoreType.DMA((9, 2)),
        pltpu.SemaphoreType.DMA((8, 2)),
        pltpu.SemaphoreType.DMA((8, 2)),
        pltpu.SemaphoreType.DMA((2,)),
        pltpu.SemaphoreType.DMA((2,)),
    ]
    turned, zones = pl.pallas_call(
        functools.partial(kernel, rows, cols, scale),
        out_shape=(
            jax.ShapeDtypeStruct((slab_x, slab_y, depth), BF),
            jax.ShapeDtypeStruct((8, depth), F32),
        ),
        in_specs=[pl.BlockSpec(memory_space=pl.ANY)] * 8,
        out_specs=(
            pl.BlockSpec(memory_space=pl.ANY),
            pl.BlockSpec(memory_space=pltpu.VMEM),
        ),
        scratch_shapes=scratch,
        compiler_params=pltpu.CompilerParams(
            collective_id=0, has_side_effects=True, vmem_limit_bytes=56 << 20
        ),
        name="adjoint_lines",
    )(
        head_start, cotangent, conductivity, line_x, line_y, line_z, zone_map,
        owner_order.reshape(groups, depth),
    )
    vmem = pl.BlockSpec(memory_space=pltpu.VMEM)
    return pl.pallas_call(
        finish,
        out_shape=(
            jax.ShapeDtypeStruct((slab_x, slab_y, depth), BF),
            jax.ShapeDtypeStruct((zone_count // (rows * cols),), F32),
        ),
        in_specs=[vmem, vmem],
        out_specs=(vmem, vmem),
        name="finish_slab",
    )(turned, zones)


def solution(mesh):
    slab = P("row", "col", None)
    return jax.shard_map(
        functools.partial(on_device, mesh.shape["row"], mesh.shape["col"]),
        mesh=mesh,
        in_specs=(slab, slab, slab, P(), P(), P(), P(), P()),
        out_specs=(slab, P(("row", "col"))),
        check_vma=False,
    )
```

```python
import functools
import math

import jax
import jax.numpy as jnp
from jax import lax
from jax.experimental import pallas as pl
from jax.experimental.pallas import tpu as pltpu
from jax.sharding import PartitionSpec as P

MESH = pl.DeviceIdType.MESH
BF = jnp.bfloat16
F32 = jnp.float32
HALF_STEP = 0.075
PAD = 8


def dot_nn(a, b):
    return lax.dot_general(a, b, (((1,), (0,)), ((), ())), preferred_element_type=F32)


def dot_nt(a, b):
    return lax.dot_general(a, b, (((1,), (1,)), ((), ())), preferred_element_type=F32)


def dot_tn(a, b):
    return lax.dot_general(a, b, (((0,), (0,)), ((), ())), preferred_element_type=F32)


def loop(count, body, unroll=1):
    def step(i, carry):
        body(i)
        return carry

    lax.fori_loop(0, count, step, 0, unroll=unroll)


def split_two(values):
    high = values.astype(BF)
    low = (values - high.astype(F32)).astype(BF)
    return high, low


def kernel(
    rows, cols, scale,
    head_hbm, cot_hbm, cond_hbm, lx_hbm, ly_hbm, lz_hbm, zmap_hbm, owner_hbm,
    out_ref, zout_ref,
    head, cond, lx, ly, lz, zone_block, zone_turned, zone_y, owner,
    rs, rr, cs, cr, turn, cfx, cfy, cfz_y,
    field0, field3, grad3, grad0, field1, field4, grad4, grad1,
    back5, back2, state2, state5, src_x, src_y,
    zone_cols, zone_lines, lo_x, lo_y, lo_own, hi_own, spread_x, spread_y,
    zacc, z_send, z_mid, z_row, z_col,
    local_sem, rs_sem, rr_sem, cs_sem, cr_sem, zs_sem, zr_sem,
):
    row = lax.axis_index("row")
    col = lax.axis_index("col")
    slab_x, slab_y, depth = head_hbm.shape
    part_x = slab_x // cols
    total_x = lx.shape[0]
    total_y = ly.shape[0]
    half_y = slab_y // 2
    piece_y = half_y // rows

    def row_peer(i):
        return lax.rem(row + i, rows)

    def col_peer(i):
        return lax.rem(col + i, cols)

    barrier = pltpu.get_barrier_semaphore()

    def greet_row(i):
        pl.semaphore_signal(barrier, inc=1, device_id=(row_peer(i + 1), col), device_id_type=MESH)

    def greet_col(i):
        pl.semaphore_signal(barrier, inc=1, device_id=(row, col_peer(i + 1)), device_id_type=MESH)

    loop(rows - 1, greet_row, rows - 1)
    loop(cols - 1, greet_col, cols - 1)

    loads = {}

    def load(slot, src, dst):
        copy = pltpu.make_async_copy(src, dst, local_sem.at[slot])
        copy.start()
        loads[slot] = copy

    own_x = pl.ds(col * part_x, part_x)
    load(0, cond_hbm, cond)
    load(1, head_hbm, head)

    def near_last(k, count):
        return count // 2 + ((k + 1) // 2) * (1 - 2 * lax.rem(k, 2))

    ring_x = 4
    side = lax.rem(col, 2)
    ring_z = rows // ring_x

    def send_row(k, h):
        def one(shift_z, shift_x):
            z = lax.rem(row // ring_x + shift_z + side * (ring_z - 2 * shift_z), ring_z)
            x = lax.rem(lax.rem(row, ring_x) + shift_x + side * (ring_x - 2 * shift_x), ring_x)
            r = z * ring_x + x
            pltpu.make_async_remote_copy(
                src_ref=rs.at[k, h, r], dst_ref=rr.at[k, h, row],
                send_sem=rs_sem.at[k, h], recv_sem=rr_sem.at[k, h],
                device_id=(r, col), device_id_type=MESH,
            ).start()

        shifts_z = [ring_z // 2 + ((i + 1) // 2) * (1 - 2 * (i % 2)) for i in range(ring_z)]

        def lines(i):
            for shift_z in shifts_z:
                one(shift_z, near_last(i, ring_x))

        loop(ring_x - 1, lines)
        for shift_z in shifts_z[:-1]:
            one(shift_z, 0)
        rr[k, h, row] = rs[k, h, row]

    def row_wait(k, h):
        part = pl.ds(0, rows - 1)
        return pltpu.make_async_remote_copy(
            src_ref=rs.at[k, h, part], dst_ref=rr.at[k, h, part],
            send_sem=rs_sem.at[k, h], recv_sem=rr_sem.at[k, h],
            device_id=(row, col), device_id_type=MESH,
        )

    all_y = pl.ds(0, slab_y)

    def half(h):
        return pl.ds(h * half_y, half_y)

    def send_col(j, slot, src, ys):
        def one(i):
            c = col_peer(i + 1)
            pltpu.make_async_remote_copy(
                src_ref=src.at[pl.ds(c * part_x, part_x), ys],
                dst_ref=cr.at[j, own_x, ys],
                send_sem=cs_sem.at[j, slot], recv_sem=cr_sem.at[j, slot],
                device_id=(row, c), device_id_type=MESH,
            ).start()

        loop(cols - 1, one)

    def keep_own(j, src, ys):
        cr[j, own_x, ys] = src[own_x, ys]

    def col_wait(j, slot, ys):
        part = pl.ds(0, (cols - 1) * part_x)
        return pltpu.make_async_remote_copy(
            src_ref=cr.at[j, part, ys], dst_ref=cr.at[j, part, ys],
            send_sem=cs_sem.at[j, slot], recv_sem=cr_sem.at[j, slot],
            device_id=(row, col), device_id_type=MESH,
        )

    def next_lane(f):
        return pltpu.roll(f, f.shape[1] - 1, axis=1)

    def prev_lane(f):
        return pltpu.roll(f, 1, axis=1)

    def apply_z(f, faces):
        flux = faces * (next_lane(f) - f)
        return f + flux - prev_lane(flux)

    def lane_mask(shape):
        lane = lax.broadcasted_iota(jnp.int32, shape, 1)
        return jnp.where(lane < depth - 1, 1.0, 0.0).astype(F32)

    ones8 = jnp.ones((8, 2 * depth), BF)

    def depth_sum(products):
        high, low = split_two(products)
        return dot_nt(ones8, jnp.concatenate([high, low], axis=1))

    def turn_in(x, h, plane):
        turn[pl.ds(h * half_y * slab_x + x, half_y, stride=slab_x), :] = plane

    def turn_out(x, h):
        return turn[pl.ds(h * half_y * slab_x + x, half_y, stride=slab_x), :]

    group = 4
    block = group * piece_y * slab_x

    def turned_to_send(k, h):
        def one(g):
            base = pl.multiple_of(h * half_y * slab_x + g * block, block)
            piece = turn[pl.ds(base, block), :].astype(BF)
            rs[k, h, pl.ds(g * group, group)] = piece.reshape(group, piece_y, slab_x, depth)

        loop(rows // group, one, 2)

    def received_to_turn(k, h):
        def one(g):
            base = pl.multiple_of(h * half_y * slab_x + g * block, block)
            piece = rr[k, h, pl.ds(g * group, group)].reshape(block, depth)
            turn[pl.ds(base, block), :] = piece.astype(F32)

        loop(rows // group, one, 2)

    def received_to_planes(k, h, buf, offset):
        received_to_turn(k, h)

        def one(x):
            buf[offset + x, half(h)] = turn_out(x, h).astype(BF)

        loop(slab_x, one, 4)

    def half_planes_to_send(buf, k, h):
        def one(x):
            turn_in(x, h, buf[x, half(h)].astype(F32))

        loop(slab_x, one, 4)
        turned_to_send(k, h)

    def hub_planes_to_send(buf, k):
        for h in range(2):
            half_planes_to_send(buf, k, h)

    def hub_to_lines(k, j, h):
        buf = cs.at[j]
        received_to_planes(k, h, buf, 0)
        send_col(j, h, buf, half(h))
        keep_own(j, buf, half(h))

    chunk = 128
    peers_chunk = chunk // slab_x
    chunks_x = total_x // chunk

    def received_x(k, h, y, c):
        return rr[k, h, pl.ds(c * peers_chunk, peers_chunk), y].reshape(chunk, depth)

    def to_send_x(k, h, y, c, values):
        rs[k, h, pl.ds(c * peers_chunk, peers_chunk), y] = values.astype(BF).reshape(
            peers_chunk, slab_x, depth
        )

    def rows_of(c):
        return pl.ds(pl.multiple_of(PAD + c * chunk, 8), chunk)

    def each_x(body, unroll=1):
        def one(c):
            for y in range(piece_y):
                body(y, c)

        loop(chunks_x, one, unroll)

    def pad_lines_x(field, h):
        for y in range(piece_y):
            pad_line(field, h * piece_y + y, total_x)

    def received_to_field_x(k, h, field):
        def one(y, c):
            field[h * piece_y + y, rows_of(c), :] = received_x(k, h, y, c).astype(F32)

        each_x(one)
        pad_lines_x(field, h)

    def src_part(c):
        return pl.ds(pl.multiple_of(c * chunk, chunk), chunk)

    def forward_x(k_in, k_out, h, field):
        received_to_field_x(k_in, h, field)

        def source(y, c):
            src_x[src_part(c), y * depth:(y + 1) * depth] = apply_lines(
                field, cfx, h * piece_y + y, c
            ).astype(BF)

        each_x(source)

        def line(c):
            res = dot_nn(lx[src_part(c), :], src_x[...])
            for y in range(piece_y):
                to_send_x(k_out, h, y, c, res[:, y * depth:(y + 1) * depth])

        loop(chunks_x, line, 2)
        send_row(k_out, h)

    def back_x(k_in, h, grad):
        rhs = jnp.concatenate(
            [rr[k_in, h, :, y].reshape(total_x, depth) for y in range(piece_y)], axis=1
        )

        def line(c):
            res = dot_tn(lx[:, src_part(c)], rhs)
            for y in range(piece_y):
                grad[h * piece_y + y, rows_of(c), :] = res[:, y * depth:(y + 1) * depth]

        loop(chunks_x, line, 2)
        pad_lines_x(grad, h)

    def flux_x(k_out, h, grad):
        def flux(y, c):
            to_send_x(k_out, h, y, c, apply_lines(grad, cfx, h * piece_y + y, c))

        each_x(flux)
        send_row(k_out, h)

    def adjoint_x(k_in, k_out, h, grad):
        back_x(k_in, h, grad)
        flux_x(k_out, h, grad)

    y_chunk = 256
    blocks = y_chunk // slab_y

    def line_y_chunk(m, transpose):
        part = pl.ds(pl.multiple_of(m * y_chunk, y_chunk), y_chunk)
        if transpose:
            return dot_tn(ly[:, part], src_y[...])
        return dot_nn(ly[part, :], src_y[...])

    def line_y_to_field(field):
        def one(m):
            res = line_y_chunk(m, True)
            for x in range(part_x):
                field[x, pl.ds(pl.multiple_of(PAD + m * y_chunk, 8), y_chunk), :] = res[
                    :, x * depth:(x + 1) * depth
                ]

        loop(total_y // y_chunk, one)
        pad_field(field)

    def line_y_to_blocks(body):
        def one(m):
            res = line_y_chunk(m, False).astype(BF)
            for b in range(blocks):
                for x in range(part_x):
                    body(
                        (m * blocks + b) * part_x + x,
                        res[b * slab_y:(b + 1) * slab_y, x * depth:(x + 1) * depth],
                    )

        loop(total_y // y_chunk, one)

    def pad_line(field, line, length):
        field[line, 0:PAD, :] = jnp.broadcast_to(field[line, PAD:PAD + 1, :], (PAD, depth))
        field[line, PAD + length:, :] = jnp.broadcast_to(
            field[line, PAD + length - 1:PAD + length, :], (PAD, depth)
        )

    def pad_field(field):
        for x in range(part_x):
            pad_line(field, x, total_y)

    def received_to_field(j, field):
        def one(c):
            for x in range(part_x):
                field[x, pl.ds(pl.multiple_of(PAD + c * slab_y, 8), slab_y), :] = cr[
                    j, c * part_x + x
                ].astype(F32)

        loop(cols, one, 2)
        pad_field(field)

    def three(field, x, c):
        base = pl.multiple_of(PAD + c * slab_y, 8)
        return (
            field[x, pl.ds(base - 1, slab_y), :],
            field[x, pl.ds(base, slab_y), :],
            field[x, pl.ds(base + 1, slab_y), :],
        )

    def apply_lines(field, faces, x, c):
        below, mid, above = three(field, x, c)
        face_below, face, _ = three(faces, x, c)
        return mid + face * (above - mid) - face_below * (mid - below)

    def apply_y(field, x, c):
        return apply_lines(field, cfy, x, c)

    def cells_line(field, grad, x, c):
        below, mid, above = three(field, x, c)
        g_below, g_mid, g_above = three(grad, x, c)
        return (above - mid) * (g_above - g_mid) + (mid - below) * (g_mid - g_below)

    def faces_line(field, faces, x, c):
        _, mid, above = three(field, x, c)
        faces[x, rows_of(c), :] = HALF_STEP * (mid + above)

    def close_faces(faces, x, length):
        faces[x, 0:PAD, :] = jnp.zeros((PAD, depth), F32)
        faces[x, PAD + length - 1:PAD + length, :] = jnp.zeros((1, depth), F32)
        faces[x, PAD + length:, :] = jnp.zeros((PAD, depth), F32)

    def cells_z(state, backed):
        first = next_lane(state) - state
        second = next_lane(backed) - backed
        return 2.0 * first * second * lane_mask(state.shape)

    def set_src_y(x, c, values):
        src_y[pl.ds(pl.multiple_of(c * slab_y, slab_y), slab_y), x * depth:(x + 1) * depth] = (
            values.astype(BF)
        )

    def source_y(field):
        def one(c):
            for x in range(part_x):
                set_src_y(x, c, apply_y(field, x, c))

        loop(cols, one, 2)

    def low_codes(zones):
        code = jnp.broadcast_to(zones & (depth - 1), (depth, depth))
        return jnp.where(
            code == lax.broadcasted_iota(jnp.int32, (depth, depth), 0), 1.0, 0.0
        ).astype(BF)

    def high_codes(zones):
        code = jnp.broadcast_to(zones // depth, (16, depth))
        return jnp.where(code == lax.broadcasted_iota(jnp.int32, (16, depth), 0), 1.0, 0.0)

    def spread(sums, zones):
        both = jnp.concatenate([sums, sums], axis=0) * high_codes(zones)
        high, low = split_two(both)
        return jnp.concatenate([high, low], axis=0)

    def lanes(index):
        return pl.ds(pl.multiple_of(index * depth, depth), depth)

    def set_codes():
        groups = 8 // part_x
        for x in range(part_x):
            line = jnp.zeros((1, total_y), jnp.int32)
            for g in range(groups):
                mine = jnp.where(lax.rem(col, groups) == g, 1, 0)
                line = line + mine * zone_y[g * part_x + x:g * part_x + x + 1, :]
            for c in range(cols):
                index = c * part_x + x
                zone_lines[index:index + 1, :] = line[:, c * slab_y:(c + 1) * slab_y]
        for c in range(chunks_x):
            block = zone_block[c * chunk:(c + 1) * chunk, :].astype(F32)
            zone_turned[c] = jnp.transpose(block)
        for h in range(2):
            for y in range(piece_y):
                for c in range(chunks_x):
                    index = (h * piece_y + y) * chunks_x + c
                    place = pl.ds(h * half_y + row * piece_y + y, 1)
                    zone_cols[index:index + 1, :] = zone_turned[c, place, :].astype(jnp.int32)

        def one(i):
            lo_x[:, lanes(i)] = low_codes(zone_cols[pl.ds(i, 1), :])
            lo_y[:, lanes(i)] = low_codes(zone_lines[pl.ds(i, 1), :])
            own = owner[pl.ds(i, 1), :]
            lo_own[:, lanes(i)] = low_codes(own)
            hi_own[:, lanes(i)] = high_codes(own)

        loop(16, one)

    def zones_x(field, grad, h):
        def one(c):
            for y in range(piece_y):
                line = h * piece_y + y
                index = line * chunks_x + c
                spread_x[:, lanes(index)] = spread(
                    depth_sum(cells_line(field, grad, line, c)), zone_cols[pl.ds(index, 1), :]
                )

        loop(chunks_x, one, 4)
        count = piece_y * chunks_x * depth
        part = slice(h * count, (h + 1) * count)
        zacc[...] += dot_nt(spread_x[:, part], lo_x[:, part])

    def zones_y(field, grad, state, back):
        def one(c):
            for x in range(part_x):
                index = c * part_x + x
                cells = cells_line(field, grad, x, c)
                cells = cells + cells_z(state[index].astype(F32), back[index])
                spread_y[:, lanes(index)] = spread(
                    depth_sum(cells), zone_lines[pl.ds(index, 1), :]
                )

        loop(cols, one, 4)
        zacc[...] += dot_nt(spread_y[...], lo_y[...])

    def back_z(j, back):
        def one(c):
            for x in range(part_x):
                index = c * part_x + x
                backed = dot_nn(cr[j, index], lz[...])
                back[index] = backed
                set_src_y(x, c, apply_z(backed, cfz_y[index]))

        loop(cols, one, 2)

    def back_y(j, grad):
        line_y_to_field(grad)

        def one(c):
            for x in range(part_x):
                cs[j, c * part_x + x] = apply_y(grad, x, c).astype(BF)

        loop(cols, one)
        send_col(j, 0, cs.at[j], all_y)
        keep_own(j, cs.at[j], all_y)

    loads[0].wait()
    half_planes_to_send(cond, 0, 0)
    pl.semaphore_wait(barrier, rows + cols - 2)
    send_row(0, 0)
    loads[1].wait()
    half_planes_to_send(head, 1, 0)
    send_row(1, 0)
    load(2, cond_hbm.at[own_x], cr.at[0, own_x])
    load(3, cot_hbm.at[own_x], cr.at[1, own_x])
    load(4, lz_hbm, lz)
    load(5, lx_hbm, lx)
    load(6, ly_hbm, ly)
    load(7, zmap_hbm.at[:, pl.ds(pl.multiple_of(col * slab_y, slab_y), slab_y)], zone_block)
    load(8, zmap_hbm.at[pl.ds(row * slab_x + (col * part_x // 8) * 8, 8)], zone_y)
    load(9, owner_hbm, owner)
    send_col(0, 0, cond_hbm, all_y)
    send_col(1, 0, cot_hbm, all_y)
    half_planes_to_send(cond, 0, 1)
    send_row(0, 1)
    half_planes_to_send(head, 1, 1)
    send_row(1, 1)

    for slot in (2, 3, 4, 5, 6):
        loads[slot].wait()
    col_wait(0, 0, all_y).wait_recv()
    received_to_field(0, field1)

    def faces_y(c):
        for x in range(part_x):
            index = c * part_x + x
            own = cr[0, index].astype(F32)
            cfz_y[index] = HALF_STEP * (own + next_lane(own)) * lane_mask(own.shape)
            faces_line(field1, cfy, x, c)

    loop(cols, faces_y)
    for x in range(part_x):
        close_faces(cfy, x, total_y)
    col_wait(1, 0, all_y).wait_recv()
    back_z(1, back5)
    back_y(2, grad4)

    zacc[...] = jnp.zeros(zacc.shape, F32)
    for h in range(2):
        row_wait(0, h).wait_recv()
        received_to_field_x(0, h, field3)

        def faces_x(y, c):
            faces_line(field3, cfx, h * piece_y + y, c)

        each_x(faces_x)
        for y in range(piece_y):
            close_faces(cfx, h * piece_y + y, total_x)
        row_wait(1, h).wait_recv()
        forward_x(1, 2, h, field0)
    for slot in (7, 8, 9):
        loads[slot].wait()
    set_codes()

    col_wait(2, 0, all_y).wait_recv()
    hub_planes_to_send(cr.at[2], 3)
    for h in range(2):
        row_wait(2, h).wait_recv()
        send_row(3, h)
        hub_to_lines(2, 3, h)

    row_wait(3, 0).wait_recv()
    adjoint_x(3, 4, 0, grad3)

    for h in range(2):
        col_wait(3, h, half(h)).wait_recv()
    received_to_field(3, field1)
    source_y(field1)

    def state3_block(index, state):
        state2[index] = state
        source = apply_z(state.astype(F32), cfz_y[index]).astype(BF)
        cs[4, index] = dot_nt(source, lz[...]).astype(BF)

    line_y_to_blocks(state3_block)
    send_col(4, 0, cs.at[4], all_y)
    keep_own(4, cs.at[4], all_y)

    row_wait(3, 1).wait_recv()
    adjoint_x(3, 4, 1, grad3)
    col_wait(4, 0, all_y).wait_recv()
    hub_planes_to_send(cr.at[4], 5)

    for h in range(2):
        row_wait(4, h).wait_recv()
        send_row(5, h)
        hub_to_lines(4, 5, h)

    row_wait(5, 0).wait_recv()
    forward_x(5, 6, 0, field3)

    for h in range(2):
        col_wait(5, h, half(h)).wait_recv()
    back_z(5, back2)
    back_y(6, grad1)

    row_wait(5, 1).wait_recv()
    forward_x(5, 6, 1, field3)
    zones_x(field3, grad3, 0)
    zones_x(field3, grad3, 1)
    col_wait(6, 0, all_y).wait_recv()
    hub_planes_to_send(cr.at[6], 7)

    for h in range(2):
        row_wait(6, h).wait_recv()
        send_row(7, h)
        hub_to_lines(6, 7, h)
    zones_y(field1, grad1, state2, back2)

    row_wait(7, 0).wait_recv()
    adjoint_x(7, 8, 0, grad0)
    zones_x(field0, grad0, 0)

    for h in range(2):
        col_wait(7, h, half(h)).wait_recv()
    received_to_field(7, field4)
    source_y(field4)

    def state5_block(index, state):
        state5[index] = state

    line_y_to_blocks(state5_block)
    zones_y(field4, grad4, state5, back5)

    row_wait(7, 1).wait_recv()
    back_x(7, 1, grad0)
    zones_x(field0, grad0, 1)

    def leave(h):
        received_to_planes(8, h, cs.at[0], 0)
        load(10 + h, cs.at[0, :, half(h)], out_ref.at[:, half(h)])

    sums = (zacc[0:16, :] + zacc[16:32, :]) * (-HALF_STEP * scale)
    high, low = split_two(sums)
    ordered = dot_nn(jnp.concatenate([high, low], axis=0), lo_own[...])
    ordered = (ordered[0:16] + ordered[16:32]) * hi_own[...]
    ordered = jnp.sum(ordered, axis=0, keepdims=True)
    for g in range(z_send.shape[0]):
        z_send[g] = ordered[:, g * depth:(g + 1) * depth]

    def send_zone_row(i):
        r = row_peer(i + 1)
        pltpu.make_async_remote_copy(
            src_ref=z_send.at[r // 2], dst_ref=z_row.at[row],
            send_sem=zs_sem.at[0], recv_sem=zr_sem.at[0],
            device_id=(r, col), device_id_type=MESH,
        ).start()

    loop(rows - 1, send_zone_row)
    z_row[row] = z_send[row // 2]
    flux_x(8, 1, grad0)

    def zone_wait(phase, ref, count):
        part = pl.ds(0, count)
        return pltpu.make_async_remote_copy(
            src_ref=ref.at[part], dst_ref=ref.at[part],
            send_sem=zs_sem.at[phase], recv_sem=zr_sem.at[phase],
            device_id=(row, col), device_id_type=MESH,
        )

    zone_wait(0, z_row, rows - 1).wait_recv()
    z_mid[...] = jnp.sum(z_row[...], axis=0)

    def send_zone_col(i):
        c = col_peer(i + 1)
        pltpu.make_async_remote_copy(
            src_ref=z_mid, dst_ref=z_col.at[col],
            send_sem=zs_sem.at[1], recv_sem=zr_sem.at[1],
            device_id=(row, c), device_id_type=MESH,
        ).start()

    loop(cols - 1, send_zone_col)
    z_col[col] = z_mid[...]
    row_wait(8, 0).wait_recv()
    leave(0)
    zone_wait(1, z_col, cols - 1).wait_recv()
    final = jnp.sum(z_col[...], axis=0)
    offset = lax.rem(row, 2) * (depth // 2) + col * 8
    final = jnp.broadcast_to(final, zout_ref.shape)
    zout_ref[...] = pltpu.roll(final, lax.rem(depth - offset, depth), axis=1)
    row_wait(8, 1).wait_recv()
    leave(1)
    for h in range(2):
        loads[10 + h].wait()

    for k in range(9):
        for h in range(2):
            row_wait(k, h).wait_send()
    for j in (0, 1, 2, 4, 6):
        col_wait(j, 0, all_y).wait_send()
    for j in (3, 5, 7):
        for h in range(2):
            col_wait(j, h, half(h)).wait_send()
    zone_wait(0, z_row, rows - 1).wait_send()
    zone_wait(1, z_col, cols - 1).wait_send()


def finish(slab_ref, zones_ref, out_ref, zout_ref):
    out_ref[...] = slab_ref[...]
    zout_ref[...] = zones_ref[0, 0:zout_ref.shape[0]]


def on_device(
    rows, cols, head_start, cotangent, conductivity, line_x, line_y, line_z, zone_map, owner_order
):
    slab_x, slab_y, depth = head_start.shape
    total_x, total_y = zone_map.shape
    zone_count = owner_order.shape[0]
    part_x = slab_x // cols
    part_y = slab_y // rows
    scale = 1.0 / math.sqrt(total_x * total_y * depth / zone_count)
    groups = zone_count // depth
    lines_x = pltpu.VMEM((part_y, total_x + 2 * PAD, depth), F32)
    lines_y = pltpu.VMEM((part_x, total_y + 2 * PAD, depth), F32)
    slab16 = pltpu.VMEM((slab_x, slab_y, depth), BF)
    slab32 = pltpu.VMEM((slab_x, slab_y, depth), F32)
    codes = pltpu.VMEM((depth, slab_x * slab_y), BF)
    spread = pltpu.VMEM((32, slab_x * slab_y), BF)
    row_slots = pltpu.VMEM((9, 2, rows, part_y // 2, slab_x, depth), BF)
    col_slots = pltpu.VMEM((8, slab_x, slab_y, depth), BF)
    scratch = [
        slab16, slab16,
        pltpu.VMEM(line_x.shape, BF),
        pltpu.VMEM(line_y.shape, BF),
        pltpu.VMEM(line_z.shape, BF),
        pltpu.VMEM((total_x, slab_y), jnp.int32),
        pltpu.VMEM((total_x // 128, slab_y, 128), F32),
        pltpu.VMEM((8, total_y), jnp.int32),
        pltpu.VMEM((groups, depth), jnp.int32),
        row_slots, row_slots, col_slots, col_slots,
        pltpu.VMEM((slab_x * slab_y + slab_x, depth), F32),
        lines_x, lines_y, slab32,
        lines_x, lines_x, lines_x, lines_x,
        lines_y, lines_y, lines_y, lines_y,
        slab32, slab32, slab16, slab16,
        pltpu.VMEM((total_x, part_y // 2 * depth), BF),
        pltpu.VMEM((total_y, part_x * depth), BF),
        pltpu.VMEM((16, depth), jnp.int32),
        pltpu.VMEM((16, depth), jnp.int32),
        codes, codes, codes,
        pltpu.VMEM((16, zone_count), F32),
        spread, spread,
        pltpu.VMEM((32, depth), F32),
        pltpu.VMEM((groups, 1, depth), F32),
        pltpu.VMEM((1, depth), F32),
        pltpu.VMEM((rows, 1, depth), F32),
        pltpu.VMEM((cols, 1, depth), F32),
        pltpu.SemaphoreType.DMA((12,)),
        pltpu.SemaphoreType.DMA((9, 2)),
        pltpu.SemaphoreType.DMA((9, 2)),
        pltpu.SemaphoreType.DMA((8, 2)),
        pltpu.SemaphoreType.DMA((8, 2)),
        pltpu.SemaphoreType.DMA((2,)),
        pltpu.SemaphoreType.DMA((2,)),
    ]
    turned, zones = pl.pallas_call(
        functools.partial(kernel, rows, cols, scale),
        out_shape=(
            jax.ShapeDtypeStruct((slab_x, slab_y, depth), BF),
            jax.ShapeDtypeStruct((8, depth), F32),
        ),
        in_specs=[pl.BlockSpec(memory_space=pl.ANY)] * 8,
        out_specs=(
            pl.BlockSpec(memory_space=pl.ANY),
            pl.BlockSpec(memory_space=pltpu.VMEM),
        ),
        scratch_shapes=scratch,
        compiler_params=pltpu.CompilerParams(
            collective_id=0, has_side_effects=True, vmem_limit_bytes=56 << 20
        ),
        name="adjoint_lines",
    )(
        head_start, cotangent, conductivity, line_x, line_y, line_z, zone_map,
        owner_order.reshape(groups, depth),
    )
    vmem = pl.BlockSpec(memory_space=pltpu.VMEM)
    return pl.pallas_call(
        finish,
        out_shape=(
            jax.ShapeDtypeStruct((slab_x, slab_y, depth), BF),
            jax.ShapeDtypeStruct((zone_count // (rows * cols),), F32),
        ),
        in_specs=[vmem, vmem],
        out_specs=(vmem, vmem),
        name="finish_slab",
    )(turned, zones)


def solution(mesh):
    slab = P("row", "col", None)
    return jax.shard_map(
        functools.partial(on_device, mesh.shape["row"], mesh.shape["col"]),
        mesh=mesh,
        in_specs=(slab, slab, slab, P(), P(), P(), P(), P()),
        out_specs=(slab, P(("row", "col"))),
        check_vma=False,
    )
```
